256 devices in a mesh: seq: 128 (over x, y_hi, z, core), section: 2 (over y_lo).
Axes of the slice: x: 4, y: 4 (y_hi: 2, y_lo: 2; y = y_hi * 2 + y_lo), z: 8, core: 2. Of those that a mesh axis runs over, the one named last changes fastest.
Arguments:
- hidden: bfloat16 [2, 2, 2048, 3072], P('section', None, 'seq'), may hold values from -2 to 2
- image_qkv: bfloat16 [2, 2, 2048, 3, 2048], P('section', None, 'seq'), may hold values from -6 to 6
- text_slots: bfloat16 [2, 2, 128, 3, 256, 2048], P('section', None, 'seq'), may hold values from -6 to 6
- norm_gains: float32 [2, 4, 128], P('section'), may hold values from 0.7 to 2.2
- out_weight: bfloat16 [2, 2048, 3072], P('section', 'seq'), may hold values from -0.125 to 0.125
- gate: float32 [2, 4, 3072], P('section'), may hold values from 1 to 4
- owner: int32 [4], replicated, may hold values from 0 to 127
- plan: int32 [4], replicated, may hold values from 0 to 3, each once
Outputs:
- handed: bfloat16 [2, 2, 2048, 3072], P('section', None, 'seq')
- text_attn: bfloat16 [2, 128, 2, 32, 128], P('section', 'seq')
The draws below stay inside these ranges and needn't reach their ends.
Inputs may be any that keep to these rules, and one draw needn't show every extreme that they name: `plan`: each prompt appears once.
All inputs are finite; a program needn't handle non-finite values.
Results may differ from the reference program's by a relative error of at most 0.0095.
Values may be sent and summed in bfloat16 or wider, within the bound.
A program may use at most 128 MiB of HBM per device.

```python
import math
import jax
import jax.numpy as jnp
import numpy as np
from jax import lax

D = 3072
H = 16
HEAD = 128
TXT = 256
COLS = 128
MICRO = 2
SECTIONS = 2
PROMPTS = 4
TOKENS = 2048
HD = 2048
TTG = 32
N_SEQ = 128


def with_ends(result, rng, least, top_value):
    longest = result.shape.index(max(result.shape))
    spots = []
    for shift in (0, 1):
        where = [jax.random.randint(jax.random.fold_in(rng, axis), (), 0, length) for axis, length in enumerate(result.shape)]
        where[longest] = (where[longest] + shift) % result.shape[longest]
        spots.append(tuple(where))
    return result.at[spots[0]].set(least).at[spots[1]].set(top_value)


def levels(own_key, extent, cuts, low, high):
    gain, own = 1.0, jax.random.fold_in(own_key, 6)
    for axis_at, shards_of in cuts:
        heights = jnp.exp(jax.random.uniform(jax.random.fold_in(own, axis_at), (shards_of,), jnp.float32, low / len(cuts), high / len(cuts)))
        gain = gain * jnp.repeat(heights, extent[axis_at] // shards_of).reshape([-1 if axis == axis_at else 1 for axis in range(len(extent))])
    return gain


def centred(own_key, extent, deviation, limit, pieces=(), kind=jnp.bfloat16):
    result = deviation * jax.random.normal(own_key, extent, jnp.float32)
    if pieces:
        result = result * levels(own_key, extent, pieces, -0.22, 0.18)
    return jnp.clip(result, -limit, limit).astype(kind)


def setup_inputs(seed: int = 0) -> dict:
    seeds = jax.random.split(jax.random.key(seed), 9)
    return {
        "hidden": centred(seeds[0], (SECTIONS, MICRO, TOKENS, D), 0.25, 2.0, ((0, 2), (2, 128))),
        "image_qkv": centred(seeds[1], (SECTIONS, MICRO, TOKENS, 3, HD), 1.0, 6.0, ((0, 2), (2, 128))),
        "text_slots": centred(seeds[2], (SECTIONS, MICRO, N_SEQ, 3, TXT, HD), 1.0, 6.0, ((0, 2), (2, 128))),
        "norm_gains": jnp.clip(jnp.exp(math.log(2.2) - 1.1451323 * jax.random.uniform(seeds[3], (SECTIONS, 4, HEAD), jnp.float32) ** levels(seeds[3], (SECTIONS, 4, HEAD), ((0, 2),), -0.2, 0.2)), 0.7, 2.2),
        "out_weight": centred(seeds[4], (SECTIONS, HD, D), HD ** -0.5, 0.125, ((0, 2), (1, 128))),
        "gate": jnp.clip(jnp.exp(math.log(4.0) - 1.3862944 * jax.random.uniform(seeds[5], (SECTIONS, PROMPTS, D), jnp.float32) ** levels(seeds[5], (SECTIONS, PROMPTS, D), ((0, 2),), -0.2, 0.2)), 1.0, 4.0),
        "owner": with_ends(jax.random.randint(seeds[6], (PROMPTS,), 0, N_SEQ), jax.random.fold_in(seeds[6], 1), 0, N_SEQ - 1).astype(jnp.int32),
        "plan": jax.random.permutation(seeds[7], PROMPTS).astype(jnp.int32),
    }


EPSILON = 1e-06
THETA = 10000.0

def rope_angles(head_size, row_pos, col_pos):
    time_dims = head_size // 8
    space_dims = (head_size - time_dims) // 2
    frequency = np.exp(-math.log(THETA) * np.arange(0, space_dims, 2) / space_dims).astype(np.float32)
    still_part = jnp.zeros((row_pos.shape[0], time_dims // 2), row_pos.dtype)
    angles = jnp.concatenate([still_part, row_pos[:, None] * frequency[None, :], col_pos[:, None] * frequency[None, :]], axis=1)
    return (jnp.cos(angles), jnp.sin(angles))

def normalize(raw_values, gain_vec):
    field = raw_values.astype(jnp.float32)
    return field * lax.rsqrt(lax.optimization_barrier(jnp.mean(field * field, axis=-1, keepdims=True)) + EPSILON) * gain_vec

def rotate(field, cosine, sine_table):
    half_size = field.shape[-1] // 2
    paired = field.reshape(field.shape[:-1] + (half_size, 2))
    even_part = paired[..., 0]
    odd_part = paired[..., 1]
    cos_b = cosine[:, None, :]
    sin_b = sine_table[:, None, :]
    turned = jnp.stack([even_part * cos_b - odd_part * sin_b, even_part * sin_b + odd_part * cos_b], axis=-1)
    return turned.reshape(field.shape)

def attend(queries, keys, values):
    score_scale = 1.0 / math.sqrt(queries.shape[-1])
    scores = jnp.dot(queries, keys.T, preferred_element_type=jnp.float32) * score_scale
    weights = jnp.exp(scores)
    denominator = lax.optimization_barrier(jnp.sum(weights, axis=1, keepdims=True))
    numerator = jnp.dot(weights.astype(jnp.bfloat16), values, preferred_element_type=jnp.float32)
    return (numerator / denominator).astype(jnp.bfloat16)

def attend_triple(triple_args):
    return attend(triple_args[0], triple_args[1], triple_args[2])

def reference(hidden, image_qkv, text_slots, norm_gains, out_weight, gate, owner, plan):
    positions = jnp.arange(TOKENS)
    row_pos = (positions // COLS).astype(jnp.float32)
    col_pos = (positions % COLS).astype(jnp.float32)
    cosine, sine_table = rope_angles(HEAD, row_pos, col_pos)
    blocks_all = []
    texts_all = []
    for section_index in range(SECTIONS):
        norm_gain = norm_gains[section_index]
        section_blocks = []
        section_texts = []
        for micro_index in range(MICRO):
            prompt_index = plan[section_index * MICRO + micro_index]
            owner_index = owner[prompt_index]
            text_slot = lax.dynamic_index_in_dim(text_slots[section_index, micro_index], owner_index, 0, keepdims=False)
            text_q = normalize(text_slot[0].reshape(TXT, H, HEAD), norm_gain[2]).astype(jnp.bfloat16)
            text_k = normalize(text_slot[1].reshape(TXT, H, HEAD), norm_gain[3]).astype(jnp.bfloat16)
            text_v = text_slot[2].reshape(TXT, H, HEAD)
            image_data = image_qkv[section_index, micro_index]
            image_q = rotate(normalize(image_data[:, 0].reshape(TOKENS, H, HEAD), norm_gain[0]), cosine, sine_table).astype(jnp.bfloat16)
            image_k = rotate(normalize(image_data[:, 1].reshape(TOKENS, H, HEAD), norm_gain[1]), cosine, sine_table).astype(jnp.bfloat16)
            image_v = image_data[:, 2].reshape(TOKENS, H, HEAD)
            queries = jnp.concatenate([text_q, image_q], axis=0).transpose(1, 0, 2)
            keys = jnp.concatenate([text_k, image_k], axis=0).transpose(1, 0, 2)
            values = jnp.concatenate([text_v, image_v], axis=0).transpose(1, 0, 2)
            attended_rows = lax.map(attend_triple, (queries, keys, values))
            text_out = attended_rows[:, :TXT].reshape(N_SEQ, TTG, HEAD)
            image_out = attended_rows[:, TXT:].transpose(1, 0, 2).reshape(TOKENS, HD)
            projected = jnp.dot(image_out, out_weight[section_index], preferred_element_type=jnp.float32)
            gate_row = lax.dynamic_index_in_dim(gate[section_index], prompt_index, 0, keepdims=False)
            block_out = (hidden[section_index, micro_index].astype(jnp.float32) + gate_row[None, :] * projected).astype(jnp.bfloat16)
            section_blocks.append(block_out)
            section_texts.append(text_out)
        blocks_all.append(jnp.stack(section_blocks))
        texts_all.append(jnp.stack(section_texts, axis=1))
    handed = jnp.stack([blocks_all[(section_index - 1) % SECTIONS] for section_index in range(SECTIONS)])
    return (handed, jnp.stack(texts_all))
```

```python
import functools
import math

import jax
import jax.numpy as jnp
import numpy as np
from jax import lax
from jax.experimental import pallas as pl
from jax.experimental.pallas import tpu as pltpu
from jax.sharding import PartitionSpec as P

COLS = 128
EPSILON = 1e-06
THETA = 10000.0
DIMS = (4, 2, 8)
CORES = 2
HEAD = 128
MESH = pl.DeviceIdType.MESH


def rope_table(tokens):
    rows = tokens // COLS
    time_dims = HEAD // 8
    space = (HEAD - time_dims) // 2
    frequency = np.exp(-math.log(THETA) * np.arange(0, space, 2) / space).astype(np.float32)

    def angles(count):
        at = np.arange(count, dtype=np.float32)[:, None] * frequency[None, :]
        return np.repeat(at.astype(np.float64), 2, axis=1)

    table = np.zeros((2, rows + COLS, HEAD), np.float32)
    sign = np.where(np.arange(space) % 2 == 0, -1.0, 1.0)
    table[0, :rows, :time_dims] = 1.0
    by_row = slice(time_dims, time_dims + space)
    by_col = slice(time_dims + space, HEAD)
    table[0, :rows, by_row] = np.cos(angles(rows))
    table[1, :rows, by_row] = np.sin(angles(rows)) * sign
    table[0, rows:, by_col] = np.cos(angles(COLS))
    table[1, rows:, by_col] = np.sin(angles(COLS)) * sign
    return table


def normalize(raw, gain):
    field = raw.astype(jnp.float32)
    return field * lax.rsqrt(jnp.mean(field * field, axis=-1, keepdims=True) + EPSILON) * gain


def drain(ref, sem):
    pltpu.make_async_copy(ref, ref, sem).wait()


def kernel(
    dims,
    owner_ref,
    plan_ref,
    gains_ref,
    table_ref,
    gate_ref,
    qkv_ref,
    hidden_ref,
    text_ref,
    weight_ref,
    handed_ref,
    text_out_ref,
    slots,
    stage1,
    recv1,
    stage2,
    recv2,
    text_q,
    text_kv,
    qkv_send,
    qkv_recv,
    image_kv,
    num,
    den,
    rows_out,
    text_send,
    attn,
    wts,
    hid,
    total,
    out_send,
    send,
    recv,
    local,
    chunk_send,
    chunk_recv,
    chunk_local,
    ring_send,
    ring_recv,
):
    nx, ny, nz = dims
    plane = ny * nz
    seq = lax.axis_index("seq")
    section = lax.axis_index("section")
    core = seq % CORES
    yz = (seq // CORES) % plane
    x = seq // (CORES * plane)
    y, z = yz // nz, yz % nz
    other = CORES - 1 - core
    block = x * CORES + core
    blocks = nx * CORES
    tokens = qkv_ref.shape[3]
    group = text_q.shape[0]
    half = group // CORES
    width = hid.shape[-1]
    inner = attn.shape[-1]
    scale = math.log2(math.e) / math.sqrt(HEAD)

    def at(x_, yz_, core_):
        return (x_ * plane + yz_) * CORES + core_

    def remote(src, dst, send_sem, recv_sem, where, section_=None):
        place = {"seq": where} if section_ is None else {"seq": where, "section": section_}
        pltpu.make_async_remote_copy(
            src_ref=src, dst_ref=dst, send_sem=send_sem, recv_sem=recv_sem,
            device_id=place, device_id_type=MESH,
        ).start()

    def lanes(index, size):
        return pl.ds(pl.multiple_of(index * size, size), size)

    barrier = pltpu.get_barrier_semaphore()

    def greet(where, section_=None):
        place = {"seq": where} if section_ is None else {"seq": where, "section": section_}
        pl.semaphore_signal(barrier, inc=1, device_id=place, device_id_type=MESH)

    here = yz * CORES + core

    @pl.loop(1, plane * CORES)
    def _(i):
        greet(x * plane * CORES + lax.rem(here + i, plane * CORES))

    for dx in range(1, nx):
        for c in range(CORES):
            greet(at((x + dx) % nx, yz, c))
    for x_ in range(nx):
        for c in range(CORES):
            greet(at(x_, yz, c), 1 - section)
    per_head = nx * CORES
    for m in range(CORES):
        source = at((seq % per_head) // CORES, seq // per_head, m)

        @pl.when(source != seq)
        def _():
            greet(source)

    text_dest = [yz * per_head + CORES * x + part for part in range(CORES)]
    to_self = sum((dest == seq).astype(jnp.int32) for dest in text_dest)
    pl.semaphore_wait(
        barrier, plane * CORES - 1 + CORES * (nx - 1) + CORES * nx + CORES - to_self
    )

    order = sorted(range(nx), key=lambda d: -min(d, nx - d))
    for i, dx in enumerate(order):
        rows = lanes((x + dx) % nx, group)
        remote(
            text_ref.at[0, other, 0, :, rows, :], slots.at[core, :, rows, :],
            chunk_send.at[i], chunk_recv.at[i], at(x, yz, other),
        )
        pltpu.make_async_copy(
            text_ref.at[0, core, 0, :, rows, :], slots.at[core, :, rows, :], chunk_local.at[i]
        ).start()

    for dx in range(nx):
        for dc in range(CORES):
            x_, c_ = (x + dx) % nx, (core + dc) % CORES
            columns = lanes(x_ * CORES + c_, width)
            weight_from, weight_to = weight_ref.at[0, :, columns], wts.at[z, y, block]
            hidden_from, hidden_to = hidden_ref.at[0, :, :, columns], hid.at[block]
            if dx == 0 and dc == 0:
                pltpu.make_async_copy(weight_from, weight_to, local.at[0]).start()
                pltpu.make_async_copy(hidden_from, hidden_to, local.at[1]).start()
            else:
                remote(weight_from, weight_to, send.at[0], recv.at[0], at(x_, yz, c_))
                remote(hidden_from, hidden_to, send.at[1], recv.at[1], at(x_, yz, c_))

    first = seq * tokens
    row_line = first // COLS
    col_line = pl.multiple_of(table_ref.shape[1] - COLS + first % COLS, tokens)
    cosine = table_ref[0, pl.ds(row_line, 1), :] + table_ref[0, pl.ds(col_line, tokens), :]
    sine = table_ref[1, pl.ds(row_line, 1), :] + table_ref[1, pl.ds(col_line, tokens), :]
    even = lax.broadcasted_iota(jnp.int32, (tokens, HEAD), 1) % 2 == 0

    @pl.loop(0, plane)
    def _(head):
        span = lanes(head, HEAD)
        for m in range(CORES):
            for t in range(2):
                field = normalize(qkv_ref[0, m, t, :, span], gains_ref[0, t, :][None, :])
                swapped = jnp.where(
                    even, pltpu.roll(field, HEAD - 1, 1), pltpu.roll(field, 1, 1)
                )
                qkv_send[head, m, t] = (field * cosine + swapped * sine).astype(jnp.bfloat16)
            qkv_send[head, m, 2] = qkv_ref[0, m, 2, :, span]
            dest = at(x, head, m)

            @pl.when(dest != seq)
            def _():
                remote(
                    qkv_send.at[head, m], qkv_recv.at[here], send.at[2], recv.at[2], dest
                )

            @pl.when(dest == seq)
            def _():
                pltpu.make_async_copy(
                    qkv_send.at[head, m], qkv_recv.at[here], local.at[2]
                ).start()

    core_of = [(owner_ref[plan_ref[section * CORES + m]]) % CORES for m in range(CORES)]
    yz_of = [(owner_ref[plan_ref[section * CORES + m]] // CORES) % plane for m in range(CORES)]
    x_of = [owner_ref[plan_ref[section * CORES + m]] // (CORES * plane) for m in range(CORES)]
    pick = lambda pair: jnp.where(core == 0, pair[0], pair[1])
    own_core, own_yz, own_x = pick(core_of), pick(yz_of), pick(x_of)

    for i, dx in enumerate(order):
        x_ = (x + dx) % nx
        rows = lanes(x_, group)
        drain(slots.at[0, :, rows, :], chunk_recv.at[i])
        drain(slots.at[0, :, rows, :], chunk_local.at[i])
        for t in range(3):

            @pl.loop(0, plane)
            def _(head):
                span = lanes(head, HEAD)
                piece = jnp.where(own_core == 0, slots[0, t, rows, span], slots[1, t, rows, span])
                if dx == 0:
                    recv1[x, t, :, span] = piece
                else:
                    stage1[i, t, :, span] = piece

        if dx != 0:
            remote(stage1.at[i], recv1.at[x], send.at[3], recv.at[3], at(x_, yz, core))

    drain(qkv_recv.at[pl.ds(0, plane * CORES - 1)], recv.at[2])
    drain(qkv_recv.at[0], local.at[2])
    for dx in range(1, nx):
        remote(
            qkv_recv.at[:, pl.ds(1, 2)], image_kv.at[x], send.at[4], recv.at[4],
            at((x + dx) % nx, yz, core),
        )
    pltpu.make_async_copy(qkv_recv.at[:, pl.ds(1, 2)], image_kv.at[x], local.at[4]).start()

    drain(wts.at[0, 0, 0], local.at[0])
    drain(wts.at[0, 0, pl.ds(0, blocks - 1)], recv.at[0])
    for dy in range(1, ny):
        remote(
            wts.at[z, y], wts.at[z, y], send.at[7], recv.at[7],
            at(x, lax.rem(y + dy, ny) * nz + z, core),
        )
    drain(wts.at[0, pl.ds(0, ny - 1)], recv.at[7])

    steps = (nz // 2, (nz - 1) // 2)
    for step in range(steps[0]):
        for way, sign in enumerate((1, -1)):
            if step < steps[way]:
                slot = lax.rem(z - sign * step + nz, nz)
                remote(
                    wts.at[slot], wts.at[slot], ring_send.at[way, step],
                    ring_recv.at[way, step], at(x, y * nz + lax.rem(z + sign + nz, nz), core),
                )
        for way in range(2):
            if step < steps[way]:
                drain(wts.at[0], ring_recv.at[way, step])

    drain(recv1.at[pl.ds(0, nx - 1)], recv.at[3])

    @pl.loop(0, plane)
    def _(head):
        piece = recv1[own_x, :, :, lanes(head, HEAD)]
        stage2[head] = piece

        @pl.when(head == yz)
        def _():
            recv2[head] = piece

        @pl.when(head != yz)
        def _():
            remote(stage2.at[head], recv2.at[yz], send.at[5], recv.at[5], at(x, head, core))

    def meet(queries, keys, values):
        scores = lax.dot_general(
            queries, keys, (((1,), (1,)), ((), ())), preferred_element_type=jnp.float32
        )
        weights = jnp.exp2(scores * scale)
        part = weights[:, :HEAD]
        for k in range(1, keys.shape[0] // HEAD):
            part = part + weights[:, k * HEAD : (k + 1) * HEAD]
        return (
            jnp.dot(weights.astype(jnp.bfloat16), values, preferred_element_type=jnp.float32),
            part,
        )

    image_rows = plane * CORES * tokens
    row_block = HEAD
    sources = row_block // tokens

    def image_queries(index):
        return qkv_recv[pl.ds(index * sources, sources), 0].reshape(row_block, HEAD)

    def image_pair(x_):
        return [image_kv[x_, :, t].reshape(image_rows, HEAD) for t in range(2)]

    drain(image_kv.at[pl.ds(0, nx - 1)], recv.at[4])
    drain(image_kv.at[0], local.at[4])

    @pl.loop(0, image_rows // row_block)
    def _(index):
        queries = image_queries(index)
        parts = [meet(queries, *image_pair(x_)) for x_ in range(nx)]
        rows = lanes(index, row_block)
        num[rows, :] = sum(p[0] for p in parts[1:]) + parts[0][0]
        den[rows, :] = sum(p[1] for p in parts[1:]) + parts[0][1]

    drain(recv2.at[pl.ds(0, plane - 1)], recv.at[5])
    text_q[...] = normalize(recv2[own_yz, 0], gains_ref[0, 2, :][None, :]).astype(jnp.bfloat16)
    text_kv[x, 0] = normalize(recv2[own_yz, 1], gains_ref[0, 3, :][None, :]).astype(
        jnp.bfloat16
    )
    text_kv[x, 1] = recv2[own_yz, 2]
    for dx in range(1, nx):
        remote(
            text_kv.at[x], text_kv.at[x], send.at[6], recv.at[6], at((x + dx) % nx, yz, core)
        )
    queries = text_q[...]
    text_parts = [meet(queries, *image_pair(x_)) for x_ in range(nx)]
    drain(text_kv.at[pl.ds(0, nx - 1)], recv.at[6])
    text_pair = [text_kv[:, t].reshape(nx * group, HEAD) for t in range(2)]
    text_parts.append(meet(queries, *text_pair))

    def quotient(numerator, denominator):
        return (numerator / jnp.sum(denominator, axis=-1, keepdims=True)).astype(jnp.bfloat16)

    @pl.loop(0, image_rows // row_block)
    def _(index):
        rows = lanes(index, row_block)
        pair = [text_kv[:, t].reshape(nx * group, HEAD) for t in range(2)]
        more = meet(image_queries(index), *pair)
        rows_out[rows, :] = quotient(num[rows, :] + more[0], den[rows, :] + more[1])

    pair_rows = CORES * tokens
    own_lanes = lanes(yz, HEAD)

    @pl.loop(1, plane)
    def _(i):
        there = lax.rem(yz + i, plane)
        remote(
            rows_out.at[lanes(there, pair_rows), :], attn.at[block, :, own_lanes],
            send.at[9], recv.at[9], at(x, there, core),
        )

    attn[block, :, own_lanes] = rows_out[lanes(yz, pair_rows), :]

    text_rows = quotient(
        sum(p[0] for p in text_parts[1:]) + text_parts[0][0],
        sum(p[1] for p in text_parts[1:]) + text_parts[0][1],
    )
    for part, dest in enumerate(text_dest):
        text_send[part] = text_rows[part * half : (part + 1) * half, :]

        @pl.when(dest != seq)
        def _():
            remote(
                text_send.at[part], text_out_ref.at[0, 0, core], send.at[8], recv.at[8], dest
            )

        @pl.when(dest == seq)
        def _():
            pltpu.make_async_copy(
                text_send.at[part], text_out_ref.at[0, 0, core], local.at[8]
            ).start()

    drain(rows_out.at[pl.ds(0, (plane - 1) * pair_rows), :], recv.at[9])
    for dx in range(nx):
        for dc in range(CORES):
            if dx or dc:
                remote(
                    attn.at[block], attn.at[block], send.at[10], recv.at[10],
                    at((x + dx) % nx, yz, (core + dc) % CORES),
                )
    drain(attn.at[pl.ds(0, blocks - 1)], recv.at[10])

    depth = inner // (nx * ny)
    total[...] = jnp.zeros_like(total)

    @pl.loop(0, nx * ny)
    def _(k):
        left = attn[:, :, lanes(k, depth)].reshape(blocks * pair_rows, depth)
        right = wts[:, k % ny, pl.ds((k // ny) * CORES, CORES)].reshape(depth, width)
        total[...] += jnp.dot(left, right, preferred_element_type=jnp.float32)

    drain(hid.at[0], local.at[1])
    drain(hid.at[pl.ds(0, blocks - 1)], recv.at[1])
    columns = lanes(block, width)

    @pl.loop(0, blocks)
    def _(dest):
        x_, c_ = dest // CORES, dest % CORES
        for m in range(CORES):
            gate_row = gate_ref[0, pl.ds(plan_ref[section * CORES + m], 1), columns]
            rows = lanes((x_ * CORES + m) * CORES + c_, tokens)
            out_send[dest, m] = (
                hid[dest, m].astype(jnp.float32) + gate_row * total[rows, :]
            ).astype(jnp.bfloat16)
        remote(
            out_send.at[dest], handed_ref.at[0, :, :, columns], send.at[11], recv.at[11],
            at(x_, yz, c_), 1 - section,
        )

    drain(out_send, recv.at[11])

    @pl.when(to_self == 0)
    def _():
        drain(text_send, recv.at[8])
        drain(text_send, send.at[8])

    @pl.when(to_self != 0)
    def _():
        drain(text_send.at[0], recv.at[8])
        drain(text_send.at[0], local.at[8])
        drain(text_send.at[0], send.at[8])

    for i in range(nx):
        drain(slots.at[0, :, pl.ds(0, group), :], chunk_send.at[i])
    for step in range(steps[0]):
        for way in range(2):
            if step < steps[way]:
                drain(wts.at[0], ring_send.at[way, step])
    drain(wts.at[0, 0, pl.ds(0, blocks - 1)], send.at[0])
    drain(hid.at[pl.ds(0, blocks - 1)], send.at[1])
    drain(qkv_recv.at[pl.ds(0, plane * CORES - 1)], send.at[2])
    drain(recv1.at[pl.ds(0, nx - 1)], send.at[3])
    drain(image_kv.at[pl.ds(0, nx - 1)], send.at[4])
    drain(recv2.at[pl.ds(0, plane - 1)], send.at[5])
    drain(text_kv.at[pl.ds(0, nx - 1)], send.at[6])
    drain(wts.at[0, pl.ds(0, ny - 1)], send.at[7])
    drain(rows_out.at[pl.ds(0, (plane - 1) * pair_rows), :], send.at[9])
    drain(attn.at[pl.ds(0, blocks - 1)], send.at[10])
    drain(out_send, send.at[11])


def per_device(hidden, image_qkv, text_slots, norm_gains, out_weight, gate, owner, plan):
    nx, ny, nz = DIMS
    plane = ny * nz
    blocks = nx * CORES
    tokens, model = hidden.shape[2:]
    inner = image_qkv.shape[-1]
    text_len = text_slots.shape[4]
    group = text_len // nx
    width = model // blocks
    weight_rows = out_weight.shape[1]
    image_rows = plane * CORES * tokens
    table = jnp.asarray(rope_table(tokens * blocks * plane))
    bf16, f32 = jnp.bfloat16, jnp.float32
    vmem = pl.BlockSpec(memory_space=pltpu.VMEM)
    smem = pl.BlockSpec(memory_space=pltpu.SMEM)
    anywhere = pl.BlockSpec(memory_space=pl.ANY)
    dma = pltpu.SemaphoreType.DMA
    return pl.pallas_call(
        functools.partial(kernel, DIMS),
        out_shape=(
            jax.ShapeDtypeStruct(hidden.shape, bf16),
            jax.ShapeDtypeStruct((1, 1, CORES, group // CORES, HEAD), bf16),
        ),
        in_specs=[smem, smem, vmem, vmem, vmem, vmem, anywhere, anywhere, anywhere],
        out_specs=(anywhere, anywhere),
        scratch_shapes=[
            pltpu.VMEM((CORES, 3, text_len, inner), bf16),
            pltpu.VMEM((nx - 1, 3, group, inner), bf16),
            pltpu.VMEM((nx, 3, group, inner), bf16),
            pltpu.VMEM((plane, 3, group, HEAD), bf16),
            pltpu.VMEM((plane, 3, group, HEAD), bf16),
            pltpu.VMEM((group, HEAD), bf16),
            pltpu.VMEM((nx, 2, group, HEAD), bf16),
            pltpu.VMEM((plane, CORES, 3, tokens, HEAD), bf16),
            pltpu.VMEM((plane * CORES, 3, tokens, HEAD), bf16),
            pltpu.VMEM((nx, plane * CORES, 2, tokens, HEAD), bf16),
            pltpu.VMEM((image_rows, HEAD), f32),
            pltpu.VMEM((image_rows, HEAD), f32),
            pltpu.VMEM((image_rows, HEAD), bf16),
            pltpu.VMEM((CORES, group // CORES, HEAD), bf16),
            pltpu.VMEM((blocks, CORES * tokens, inner), bf16),
            pltpu.VMEM((nz, ny, blocks, weight_rows, width), bf16),
            pltpu.VMEM((blocks, CORES, tokens, width), bf16),
            pltpu.VMEM((blocks * CORES * tokens, width), f32),
            pltpu.VMEM((blocks, CORES, tokens, width), bf16),
            dma((12,)),
            dma((12,)),
            dma((12,)),
            dma((nx,)),
            dma((nx,)),
            dma((nx,)),
            dma((2, nz // 2)),
            dma((2, nz // 2)),
        ],
        compiler_params=pltpu.CompilerParams(
            collective_id=0, has_side_effects=True, vmem_limit_bytes=48 * 2**20
        ),
    )(
        owner,
        plan,
        norm_gains,
        table,
        gate,
        image_qkv.transpose(0, 1, 3, 2, 4),
        hidden,
        text_slots,
        out_weight,
    )


def solution(mesh):
    return jax.shard_map(
        per_device,
        mesh=mesh,
        in_specs=(
            P("section", None, "seq", None),
            P("section", None, "seq", None, None),
            P("section", None, "seq", None, None, None),
            P("section", None, None),
            P("section", "seq", None),
            P("section", None, None),
            P(),
            P(),
        ),
        out_specs=(P("section", None, "seq", None), P("section", "seq", None, None, None)),
        check_vma=False,
    )
```

```python
import functools
import math

import jax
import jax.numpy as jnp
import numpy as np
from jax import lax
from jax.experimental import pallas as pl
from jax.experimental.pallas import tpu as pltpu
from jax.sharding import PartitionSpec as P

COLS = 128
EPSILON = 1e-06
THETA = 10000.0
DIMS = (4, 2, 8)
CORES = 2
HEAD = 128
MESH = pl.DeviceIdType.MESH


def rope_table(tokens):
    rows = tokens // COLS
    time_dims = HEAD // 8
    space = (HEAD - time_dims) // 2
    frequency = np.exp(-math.log(THETA) * np.arange(0, space, 2) / space).astype(np.float32)

    def angles(count):
        at = np.arange(count, dtype=np.float32)[:, None] * frequency[None, :]
        return np.repeat(at.astype(np.float64), 2, axis=1)

    table = np.zeros((2, rows + COLS, HEAD), np.float32)
    sign = np.where(np.arange(space) % 2 == 0, -1.0, 1.0)
    table[0, :rows, :time_dims] = 1.0
    by_row = slice(time_dims, time_dims + space)
    by_col = slice(time_dims + space, HEAD)
    table[0, :rows, by_row] = np.cos(angles(rows))
    table[1, :rows, by_row] = np.sin(angles(rows)) * sign
    table[0, rows:, by_col] = np.cos(angles(COLS))
    table[1, rows:, by_col] = np.sin(angles(COLS)) * sign
    return table


def normalize(raw, gain):
    field = raw.astype(jnp.float32)
    return field * lax.rsqrt(jnp.mean(field * field, axis=-1, keepdims=True) + EPSILON) * gain


def drain(ref, sem):
    pltpu.make_async_copy(ref, ref, sem).wait()


def kernel(
    dims,
    owner_hbm,
    plan_hbm,
    gains_hbm,
    table_hbm,
    gate_hbm,
    qkv_hbm,
    hidden_ref,
    text_ref,
    weight_ref,
    handed_ref,
    text_out_ref,
    owner_ref,
    plan_ref,
    gains_ref,
    table_ref,
    gate_ref,
    qkv_ref,
    slots,
    a1_out,
    a1_0,
    a1_1,
    a1_2,
    a2_out,
    a2_0,
    a2_1,
    a2_2,
    b1_out,
    b1_0,
    b1_1,
    b1_2,
    b2_out,
    b2_0,
    b2_1,
    b2_2,
    z_out,
    z_in_0,
    z_in_1,
    z_in_2,
    text_q,
    text_kv,
    qkv_send,
    qkv_recv,
    image_kv,
    num,
    den,
    rows_out,
    text_send,
    attn,
    wts,
    hid,
    total,
    out_send,
    send,
    recv,
    local,
    t_send,
    t_recv,
    t_local,
    ring_send,
    ring_recv,
    line_recv,
):
    nx, ny, nz = dims
    plane = ny * nz
    seq = lax.axis_index("seq")
    section = lax.axis_index("section")
    core = seq % CORES
    yz = (seq // CORES) % plane
    x = seq // (CORES * plane)
    y, z = yz // nz, yz % nz
    other = CORES - 1 - core
    far = ny - 1 - y
    block = x * CORES + core
    blocks = nx * CORES
    here = yz * CORES + core
    tokens = qkv_ref.shape[2]
    group = text_q.shape[0]
    half = group // CORES
    a1, a2, b1, b2 = (a1_0, a1_1, a1_2), (a2_0, a2_1, a2_2), (b1_0, b1_1, b1_2), (b2_0, b2_1, b2_2)
    z_in = z_in_0, z_in_1, z_in_2
    rows_a, rows_b, wide = a1_0.shape[1], b1_0.shape[2], b1_0.shape[3]
    width = hid.shape[-1]
    inner = attn.shape[-1]
    scale = math.log2(math.e) / math.sqrt(HEAD)

    def at(x_, yz_, core_):
        return (x_ * plane + yz_) * CORES + core_

    def remote(src, dst, send_sem, recv_sem, where, section_=None):
        place = {"seq": where} if section_ is None else {"seq": where, "section": section_}
        pltpu.make_async_remote_copy(
            src_ref=src, dst_ref=dst, send_sem=send_sem, recv_sem=recv_sem,
            device_id=place, device_id_type=MESH,
        ).start()

    def lanes(index, size):
        return pl.ds(pl.multiple_of(index * size, size), size)

    loads = [
        (qkv_hbm.at[0], qkv_ref),
        (table_hbm, table_ref),
        (gains_hbm.at[0], gains_ref),
        (owner_hbm, owner_ref),
        (plan_hbm, plan_ref),
        (gate_hbm.at[0], gate_ref),
    ]
    loads = [
        pltpu.make_async_copy(src, dst, local.at[3 + i]) for i, (src, dst) in enumerate(loads)
    ]
    for load in loads:
        load.start()

    barrier = pltpu.get_barrier_semaphore()

    def greet(where, section_=None):
        place = {"seq": where} if section_ is None else {"seq": where, "section": section_}
        pl.semaphore_signal(barrier, inc=1, device_id=place, device_id_type=MESH)

    @pl.loop(1, plane * CORES)
    def _(i):
        greet(x * plane * CORES + lax.rem(here + i, plane * CORES))

    for dx in range(1, nx):
        for c in range(CORES):
            greet(at((x + dx) % nx, yz, c))
    for x_ in range(nx):
        for c in range(CORES):
            greet(at(x_, yz, c), 1 - section)
    per_head = nx * CORES
    for m in range(CORES):
        source = at((seq % per_head) // CORES, seq // per_head, m)

        @pl.when(source != seq)
        def _():
            greet(source)

    text_dest = [yz * per_head + CORES * x + part for part in range(CORES)]
    to_self = sum((dest == seq).astype(jnp.int32) for dest in text_dest)

    for load in loads:
        load.wait()
    own = owner_ref[plan_ref[section * CORES + core]]
    own_core, own_yz, own_x = own % CORES, (own // CORES) % plane, own // (CORES * plane)
    own_y, own_z = own_yz // nz, own_yz % nz

    pl.semaphore_wait(
        barrier, plane * CORES - 1 + CORES * (nx - 1) + CORES * nx + CORES - to_self
    )

    order = (1, 2, 0)
    for t in order:
        remote(
            text_ref.at[0, other, 0, t], slots.at[core, t], t_send.at[0, t], t_recv.at[0, t],
            at(x, yz, other),
        )
        pltpu.make_async_copy(
            text_ref.at[0, core, 0, t], slots.at[core, t], t_local.at[t]
        ).start()

    def spread(t):
        drain(slots.at[0, t], t_recv.at[0, t])
        drain(slots.at[0, t], t_local.at[t])

        def fill(dst, row, count, lane, size):
            chunk = min(size, 512)

            @pl.loop(0, size // chunk)
            def _(k):
                span = pl.ds(pl.multiple_of(lane + k * chunk, HEAD), chunk)
                rows = pl.ds(pl.multiple_of(row, 16), count)
                dst[:, lanes(k, chunk)] = jnp.where(
                    own_core == 0, slots[0, t, rows, span], slots[1, t, rows, span]
                )

        for dx in sorted(range(nx), key=lambda d: -min(d, nx - d)):
            x_ = (x + dx) % nx
            if dx == 0:
                fill(a1[t].at[x], x_ * group, rows_a, 0, inner)
            else:
                fill(a1_out.at[t, dx - 1], x_ * group, rows_a, 0, inner)
                remote(
                    a1_out.at[t, dx - 1], a1[t].at[x], t_send.at[1, t], t_recv.at[1, t],
                    at(x_, yz, core),
                )

        @pl.loop(0, nx)
        def _(g):
            fill(b1_out.at[t, g], g * group + rows_a, rows_b, far * wide, wide)
            fill(b1[t].at[y, g], g * group + rows_a, rows_b, y * wide, wide)

        remote(
            b1_out.at[t], b1[t].at[y], t_send.at[2, t], t_recv.at[2, t],
            at(x, far * nz + z, core),
        )

    def cross(t):
        drain(a1[t].at[pl.ds(0, nx - 1)], t_recv.at[1, t])
        a2_out[t] = a1[t][own_x, :, lanes(far, wide)]
        remote(
            a2_out.at[t], a2[t].at[y], t_send.at[3, t], t_recv.at[3, t],
            at(x, far * nz + z, core),
        )
        a2[t][y] = a1[t][own_x, :, lanes(y, wide)]
        drain(b1[t].at[0], t_recv.at[2, t])
        for dx in sorted(range(nx), key=lambda d: -min(d, nx - d)):
            x_ = (x + dx) % nx
            if dx == 0:
                b2[t][x] = b1[t][own_y, x_]
            else:
                b2_out[t, dx - 1] = b1[t][own_y, x_]
                remote(
                    b2_out.at[t, dx - 1], b2[t].at[x], t_send.at[4, t], t_recv.at[4, t],
                    at(x_, yz, core),
                )

    def deal(t):
        drain(a2[t].at[0], t_recv.at[3, t])
        drain(b2[t].at[pl.ds(0, nx - 1)], t_recv.at[4, t])

        def fill(dst, z_):
            dst[pl.ds(0, rows_a), :] = a2[t][own_y, :, lanes(z_, HEAD)]
            dst[pl.ds(rows_a, rows_b), :] = b2[t][own_x, :, lanes(z_, HEAD)]

        fill(z_in[t].at[z], z)

        @pl.loop(1, nz)
        def _(dz):
            z_ = lax.rem(z + dz, nz)
            fill(z_out.at[t, z_], z_)
            remote(
                z_out.at[t, z_], z_in[t].at[z], t_send.at[5, t], t_recv.at[5, t],
                at(x, y * nz + z_, core),
            )

    def weights_start():
        for dx in range(nx):
            for dc in range(CORES):
                x_, c_ = (x + dx) % nx, (core + dc) % CORES
                columns = lanes(x_ * CORES + c_, width)
                weight_from, weight_to = weight_ref.at[0, :, columns], wts.at[z, y, block]
                if dx == 0 and dc == 0:
                    pltpu.make_async_copy(weight_from, weight_to, local.at[0]).start()
                else:
                    remote(weight_from, weight_to, send.at[0], recv.at[0], at(x_, yz, c_))

    def hidden_start():
        for dx in range(nx):
            for dc in range(CORES):
                x_, c_ = (x + dx) % nx, (core + dc) % CORES
                columns = lanes(x_ * CORES + c_, width)
                hidden_from, hidden_to = hidden_ref.at[0, :, :, columns], hid.at[block]
                if dx == 0 and dc == 0:
                    pltpu.make_async_copy(hidden_from, hidden_to, local.at[1]).start()
                else:
                    remote(hidden_from, hidden_to, send.at[1], recv.at[1], at(x_, yz, c_))

    def weights_over_y():
        drain(wts.at[0, 0, 0], local.at[0])
        drain(wts.at[0, 0, pl.ds(0, blocks - 1)], recv.at[0])
        remote(wts.at[z, y], wts.at[z, y], send.at[7], recv.at[7], at(x, far * nz + z, core))

    steps = (nz // 2, (nz - 1) // 2)

    def ring(step):
        if step == 0:
            drain(wts.at[0, 0], recv.at[7])
        for way, sign in enumerate((1, -1)):
            if 0 < step <= steps[way]:
                drain(wts.at[0], ring_recv.at[way, step - 1])
            if step < steps[way]:
                slot = lax.rem(z - sign * step + nz, nz)
                remote(
                    wts.at[slot], wts.at[slot], ring_send.at[way, step],
                    ring_recv.at[way, step], at(x, y * nz + lax.rem(z + sign + nz, nz), core),
                )

    def heads_start():
        @pl.loop(0, plane)
        def _(head):
            for m in range(CORES):
                dest = at(x, head, m)

                @pl.when(dest != seq)
                def _():
                    remote(
                        qkv_send.at[head, m], qkv_recv.at[here], send.at[2], recv.at[2], dest
                    )

                @pl.when(dest == seq)
                def _():
                    pltpu.make_async_copy(
                        qkv_send.at[head, m], qkv_recv.at[here], local.at[2]
                    ).start()

    def keys_start():
        drain(qkv_recv.at[pl.ds(0, plane * CORES - 1)], recv.at[2])
        drain(qkv_recv.at[0], local.at[2])
        for dx in range(1, nx):
            remote(
                qkv_recv.at[:, pl.ds(1, 2)], image_kv.at[x], send.at[4], recv.at[4],
                at((x + dx) % nx, yz, core),
            )
        pltpu.make_async_copy(
            qkv_recv.at[:, pl.ds(1, 2)], image_kv.at[x], local.at[2]
        ).start()

    weights_start()
    spread(order[0])
    first = seq * tokens
    row_line = first // COLS
    col_line = pl.multiple_of(table_ref.shape[1] - COLS + first % COLS, tokens)
    cosine = table_ref[0, pl.ds(row_line, 1), :] + table_ref[0, pl.ds(col_line, tokens), :]
    sine = table_ref[1, pl.ds(row_line, 1), :] + table_ref[1, pl.ds(col_line, tokens), :]
    even = lax.broadcasted_iota(jnp.int32, (tokens, HEAD), 1) % 2 == 0

    @pl.loop(0, plane)
    def _(head):
        span = lanes(head, HEAD)
        for m in range(CORES):
            for t in range(2):
                field = normalize(qkv_ref[m, t, :, span], gains_ref[t, :][None, :])
                swapped = jnp.where(
                    even, pltpu.roll(field, HEAD - 1, 1), pltpu.roll(field, 1, 1)
                )
                qkv_send[head, m, t] = (field * cosine + swapped * sine).astype(jnp.bfloat16)
            qkv_send[head, m, 2] = qkv_ref[m, 2, :, span]

    heads_start()
    weights_over_y()
    spread(order[1])
    spread(order[2])
    ring(0)
    cross(order[0])
    ring(1)
    cross(order[1])
    ring(2)
    deal(order[0])
    cross(order[2])
    ring(3)
    keys_start()
    deal(order[1])
    deal(order[2])
    hidden_start()
    for step in range(4, steps[0] + 1):
        ring(step)

    def meet(queries, keys, values):
        scores = lax.dot_general(
            queries, keys, (((1,), (1,)), ((), ())), preferred_element_type=jnp.float32
        )
        weights = jnp.exp2(scores * scale)
        part = weights[:, :HEAD]
        for k in range(1, keys.shape[0] // HEAD):
            part = part + weights[:, k * HEAD : (k + 1) * HEAD]
        return (
            jnp.dot(weights.astype(jnp.bfloat16), values, preferred_element_type=jnp.float32),
            part,
        )

    image_rows = plane * CORES * tokens
    row_block = HEAD
    sources = row_block // tokens

    def image_queries(index):
        return qkv_recv[pl.ds(index * sources, sources), 0].reshape(row_block, HEAD)

    def image_pair(x_):
        return [image_kv[x_, :, t].reshape(image_rows, HEAD) for t in range(2)]

    drain(image_kv.at[pl.ds(0, nx - 1)], recv.at[4])
    drain(image_kv.at[0], local.at[2])

    @pl.loop(0, image_rows // row_block)
    def _(index):
        queries = image_queries(index)
        parts = [meet(queries, *image_pair(x_)) for x_ in range(nx)]
        rows = lanes(index, row_block)
        num[rows, :] = sum(p[0] for p in parts[1:]) + parts[0][0]
        den[rows, :] = sum(p[1] for p in parts[1:]) + parts[0][1]

    def text_rows_of(t):
        drain(z_in[t].at[pl.ds(0, nz - 1)], t_recv.at[5, t])
        return z_in[t][own_z]

    text_kv[x, 0] = normalize(text_rows_of(1), gains_ref[3, :][None, :]).astype(jnp.bfloat16)
    text_kv[x, 1] = text_rows_of(2)
    for dx in range(1, nx):
        remote(
            text_kv.at[x], text_kv.at[x], send.at[6], recv.at[6], at((x + dx) % nx, yz, core)
        )
    text_q[...] = normalize(text_rows_of(0), gains_ref[2, :][None, :]).astype(jnp.bfloat16)
    queries = text_q[...]
    text_parts = [meet(queries, *image_pair(x_)) for x_ in range(nx)]
    drain(text_kv.at[pl.ds(0, nx - 1)], recv.at[6])

    def quotient(numerator, denominator):
        return (numerator / jnp.sum(denominator, axis=-1, keepdims=True)).astype(jnp.bfloat16)

    pair_rows = CORES * tokens
    own_lanes = lanes(yz, HEAD)

    @pl.loop(0, image_rows // row_block)
    def _(index):
        rows = lanes(index, row_block)
        pair = [text_kv[:, t].reshape(nx * group, HEAD) for t in range(2)]
        more = meet(image_queries(index), *pair)
        rows_out[rows, :] = quotient(num[rows, :] + more[0], den[rows, :] + more[1])
        for k in range(row_block // pair_rows):
            there = index * (row_block // pair_rows) + k

            @pl.when(there != yz)
            def _():
                remote(
                    rows_out.at[lanes(there, pair_rows), :], attn.at[x, core, :, own_lanes],
                    send.at[9], recv.at[9], at(x, there, core),
                )

    attn[x, core, :, own_lanes] = rows_out[lanes(yz, pair_rows), :]

    text_pair = [text_kv[:, t].reshape(nx * group, HEAD) for t in range(2)]
    text_parts.append(meet(queries, *text_pair))
    text_rows = quotient(
        sum(p[0] for p in text_parts[1:]) + text_parts[0][0],
        sum(p[1] for p in text_parts[1:]) + text_parts[0][1],
    )
    for part, dest in enumerate(text_dest):
        text_send[part] = text_rows[part * half : (part + 1) * half, :]

        @pl.when(dest != seq)
        def _():
            remote(
                text_send.at[part], text_out_ref.at[0, 0, core], send.at[8], recv.at[8], dest
            )

        @pl.when(dest == seq)
        def _():
            pltpu.make_async_copy(
                text_send.at[part], text_out_ref.at[0, 0, core], local.at[0]
            ).start()

    drain(rows_out.at[pl.ds(0, (plane - 1) * pair_rows), :], recv.at[9])
    for dx in range(1, nx):
        remote(
            attn.at[x, core], attn.at[x, core], send.at[10], line_recv.at[0, dx],
            at((x + dx) % nx, yz, core),
        )
    remote(
        attn.at[x, core], attn.at[x, core], send.at[3], line_recv.at[1, 0], at(x, yz, other)
    )
    for dx in sorted(range(1, nx), key=lambda d: min(d, nx - d)):
        x_ = (x - dx + nx) % nx
        drain(attn.at[0, 0], line_recv.at[0, dx])
        remote(
            attn.at[x_, core], attn.at[x_, core], send.at[3], line_recv.at[1, dx],
            at(x, yz, other),
        )
    for dx in range(nx):
        drain(attn.at[0, 0], line_recv.at[1, dx])

    depth = inner // (nx * ny)
    total[...] = jnp.zeros_like(total)

    @pl.loop(0, nx * ny)
    def _(k):
        left = attn[:, :, :, lanes(k, depth)].reshape(blocks * pair_rows, depth)
        right = wts[:, k % ny, pl.ds((k // ny) * CORES, CORES)].reshape(depth, width)
        total[...] += jnp.dot(left, right, preferred_element_type=jnp.float32)

    drain(hid.at[0], local.at[1])
    drain(hid.at[pl.ds(0, blocks - 1)], recv.at[1])
    columns = lanes(block, width)

    @pl.loop(0, blocks)
    def _(dest):
        x_, c_ = dest // CORES, dest % CORES
        for m in range(CORES):
            gate_row = gate_ref[pl.ds(plan_ref[section * CORES + m], 1), columns]
            rows = lanes((x_ * CORES + m) * CORES + c_, tokens)
            out_send[dest, m] = (
                hid[dest, m].astype(jnp.float32) + gate_row * total[rows, :]
            ).astype(jnp.bfloat16)
        remote(
            out_send.at[dest], handed_ref.at[0, :, :, columns], send.at[11], recv.at[11],
            at(x_, yz, c_), 1 - section,
        )

    for t in range(3):
        drain(slots.at[0, t], t_send.at[0, t])
        drain(a1[t].at[pl.ds(0, nx - 1)], t_send.at[1, t])
        drain(b1[t].at[0], t_send.at[2, t])
        drain(a2[t].at[0], t_send.at[3, t])
        drain(b2[t].at[pl.ds(0, nx - 1)], t_send.at[4, t])
        drain(z_in[t].at[pl.ds(0, nz - 1)], t_send.at[5, t])
    for step in range(steps[0]):
        for way in range(2):
            if step < steps[way]:
                drain(wts.at[0], ring_send.at[way, step])
    drain(wts.at[0, 0, pl.ds(0, blocks - 1)], send.at[0])
    drain(hid.at[pl.ds(0, blocks - 1)], send.at[1])
    drain(qkv_recv.at[pl.ds(0, plane * CORES - 1)], send.at[2])
    drain(attn.at[:, 0], send.at[3])
    drain(image_kv.at[pl.ds(0, nx - 1)], send.at[4])
    drain(text_kv.at[pl.ds(0, nx - 1)], send.at[6])
    drain(wts.at[0, 0], send.at[7])
    drain(rows_out.at[pl.ds(0, (plane - 1) * pair_rows), :], send.at[9])
    drain(attn.at[pl.ds(0, nx - 1), 0], send.at[10])
    drain(out_send, send.at[11])

    @pl.when(to_self == 0)
    def _():
        drain(text_send, recv.at[8])
        drain(text_send, send.at[8])

    @pl.when(to_self != 0)
    def _():
        drain(text_send.at[0], recv.at[8])
        drain(text_send.at[0], local.at[0])
        drain(text_send.at[0], send.at[8])

    drain(out_send, recv.at[11])


def per_device(hidden, image_qkv, text_slots, norm_gains, out_weight, gate, owner, plan):
    nx, ny, nz = DIMS
    plane = ny * nz
    blocks = nx * CORES
    tokens, model = hidden.shape[2:]
    inner = image_qkv.shape[-1]
    text_len = text_slots.shape[4]
    group = text_len // nx
    rows_a = group // 2
    rows_b = group - rows_a
    wide = inner // ny
    width = model // blocks
    weight_rows = out_weight.shape[1]
    image_rows = plane * CORES * tokens
    table = jnp.asarray(rope_table(tokens * blocks * plane))
    bf16, f32 = jnp.bfloat16, jnp.float32
    anywhere = pl.BlockSpec(memory_space=pl.ANY)
    dma = pltpu.SemaphoreType.DMA
    return pl.pallas_call(
        functools.partial(kernel, DIMS),
        out_shape=(
            jax.ShapeDtypeStruct(hidden.shape, bf16),
            jax.ShapeDtypeStruct((1, 1, CORES, group // CORES, HEAD), bf16),
        ),
        in_specs=[anywhere] * 9,
        out_specs=(anywhere, anywhere),
        scratch_shapes=[
            pltpu.SMEM(owner.shape, jnp.int32),
            pltpu.SMEM(plan.shape, jnp.int32),
            pltpu.VMEM(norm_gains.shape[1:], f32),
            pltpu.VMEM(table.shape, f32),
            pltpu.VMEM(gate.shape[1:], f32),
            pltpu.VMEM((CORES, 3, tokens, inner), bf16),
            pltpu.VMEM((CORES, 3, text_len, inner), bf16),
            pltpu.VMEM((3, nx - 1, rows_a, inner), bf16),
            *[pltpu.VMEM((nx, rows_a, inner), bf16)] * 3,
            pltpu.VMEM((3, rows_a, wide), bf16),
            *[pltpu.VMEM((ny, rows_a, wide), bf16)] * 3,
            pltpu.VMEM((3, nx, rows_b, wide), bf16),
            *[pltpu.VMEM((ny, nx, rows_b, wide), bf16)] * 3,
            pltpu.VMEM((3, nx - 1, rows_b, wide), bf16),
            *[pltpu.VMEM((nx, rows_b, wide), bf16)] * 3,
            pltpu.VMEM((3, nz, group, HEAD), bf16),
            *[pltpu.VMEM((nz, group, HEAD), bf16)] * 3,
            pltpu.VMEM((group, HEAD), bf16),
            pltpu.VMEM((nx, 2, group, HEAD), bf16),
            pltpu.VMEM((plane, CORES, 3, tokens, HEAD), bf16),
            pltpu.VMEM((plane * CORES, 3, tokens, HEAD), bf16),
            pltpu.VMEM((nx, plane * CORES, 2, tokens, HEAD), bf16),
            pltpu.VMEM((image_rows, HEAD), f32),
            pltpu.VMEM((image_rows, HEAD), f32),
            pltpu.VMEM((image_rows, HEAD), bf16),
            pltpu.VMEM((CORES, group // CORES, HEAD), bf16),
            pltpu.VMEM((nx, CORES, CORES * tokens, inner), bf16),
            pltpu.VMEM((nz, ny, blocks, weight_rows, width), bf16),
            pltpu.VMEM((blocks, CORES, tokens, width), bf16),
            pltpu.VMEM((blocks * CORES * tokens, width), f32),
            pltpu.VMEM((blocks, CORES, tokens, width), bf16),
            dma((12,)),
            dma((12,)),
            dma((12,)),
            dma((6, 3)),
            dma((6, 3)),
            dma((3,)),
            dma((2, nz // 2)),
            dma((2, nz // 2)),
            dma((2, nx)),
        ],
        compiler_params=pltpu.CompilerParams(
            collective_id=0, has_side_effects=True, vmem_limit_bytes=60 * 2**20
        ),
    )(
        owner,
        plan,
        norm_gains,
        table,
        gate,
        image_qkv.transpose(0, 1, 3, 2, 4),
        hidden,
        text_slots,
        out_weight,
    )


def solution(mesh):
    return jax.shard_map(
        per_device,
        mesh=mesh,
        in_specs=(
            P("section", None, "seq", None),
            P("section", None, "seq", None, None),
            P("section", None, "seq", None, None, None),
            P("section", None, None),
            P("section", "seq", None),
            P("section", None, None),
            P(),
            P(),
        ),
        out_specs=(P("section", None, "seq", None), P("section", "seq", None, None, None)),
        check_vma=False,
    )
```

```python
import functools
import math

import jax
import jax.numpy as jnp
import numpy as np
from jax import lax
from jax.experimental import pallas as pl
from jax.experimental.pallas import tpu as pltpu
from jax.sharding import PartitionSpec as P

COLS = 128
EPSILON = 1e-06
THETA = 10000.0
DIMS = (4, 2, 8)
CORES = 2
HEAD = 128
MESH = pl.DeviceIdType.MESH


def rope_table(tokens):
    rows = tokens // COLS
    time_dims = HEAD // 8
    space = (HEAD - time_dims) // 2
    frequency = np.exp(-math.log(THETA) * np.arange(0, space, 2) / space).astype(np.float32)

    def angles(count):
        at = np.arange(count, dtype=np.float32)[:, None] * frequency[None, :]
        return np.repeat(at.astype(np.float64), 2, axis=1)

    table = np.zeros((2, rows + COLS, HEAD), np.float32)
    sign = np.where(np.arange(space) % 2 == 0, -1.0, 1.0)
    table[0, :rows, :time_dims] = 1.0
    by_row = slice(time_dims, time_dims + space)
    by_col = slice(time_dims + space, HEAD)
    table[0, :rows, by_row] = np.cos(angles(rows))
    table[1, :rows, by_row] = np.sin(angles(rows)) * sign
    table[0, rows:, by_col] = np.cos(angles(COLS))
    table[1, rows:, by_col] = np.sin(angles(COLS)) * sign
    return table


def normalize(raw, gain):
    field = raw.astype(jnp.float32)
    return field * lax.rsqrt(jnp.mean(field * field, axis=-1, keepdims=True) + EPSILON) * gain


def drain(ref, sem):
    pltpu.make_async_copy(ref, ref, sem).wait()


def kernel(
    dims,
    owner_hbm,
    plan_hbm,
    gains_hbm,
    table_hbm,
    gate_hbm,
    qkv_hbm,
    hidden_ref,
    text_ref,
    weight_ref,
    handed_ref,
    text_out_ref,
    owner_ref,
    plan_ref,
    gains_ref,
    table_ref,
    gate_ref,
    qkv_ref,
    slots,
    a1_out_0,
    a1_out_1,
    a1_out_2,
    a1_0,
    a1_1,
    a1_2,
    a2_out_0,
    a2_out_1,
    a2_out_2,
    a2_0,
    a2_1,
    a2_2,
    b1_out_0,
    b1_out_1,
    b1_out_2,
    b1_0,
    b1_1,
    b1_2,
    b2_out_0,
    b2_out_1,
    b2_out_2,
    b2_0,
    b2_1,
    b2_2,
    z_out,
    z_in_0,
    z_in_1,
    z_in_2,
    text_q,
    text_kv,
    qkv_send,
    qkv_recv,
    image_kv,
    num,
    den,
    rows_out,
    text_send,
    attn,
    wts,
    hid,
    total,
    out_send,
    send,
    recv,
    local,
    t_send,
    t_recv,
    t_local,
    ring_send,
    ring_recv,
    line_recv,
):
    nx, ny, nz = dims
    plane = ny * nz
    seq = lax.axis_index("seq")
    section = lax.axis_index("section")
    core = seq % CORES
    yz = (seq // CORES) % plane
    x = seq // (CORES * plane)
    y, z = yz // nz, yz % nz
    other = CORES - 1 - core
    far = ny - 1 - y
    block = x * CORES + core
    blocks = nx * CORES
    here = yz * CORES + core
    tokens = qkv_ref.shape[2]
    group = text_q.shape[0]
    half = group // CORES
    a1, a2, b1, b2 = (a1_0, a1_1, a1_2), (a2_0, a2_1, a2_2), (b1_0, b1_1, b1_2), (b2_0, b2_1, b2_2)
    z_in = z_in_0, z_in_1, z_in_2
    a1_out, a2_out = (a1_out_0, a1_out_1, a1_out_2), (a2_out_0, a2_out_1, a2_out_2)
    b1_out, b2_out = (b1_out_0, b1_out_1, b1_out_2), (b2_out_0, b2_out_1, b2_out_2)
    rows_a, rows_b = [ref.shape[1] for ref in a1], [ref.shape[2] for ref in b1]
    wide = b1_0.shape[3]
    width = hid.shape[-1]
    inner = attn.shape[-1]
    scale = math.log2(math.e) / math.sqrt(HEAD)

    def at(x_, yz_, core_):
        return (x_ * plane + yz_) * CORES + core_

    def remote(src, dst, send_sem, recv_sem, where, section_=None):
        place = {"seq": where} if section_ is None else {"seq": where, "section": section_}
        pltpu.make_async_remote_copy(
            src_ref=src, dst_ref=dst, send_sem=send_sem, recv_sem=recv_sem,
            device_id=place, device_id_type=MESH,
        ).start()

    def lanes(index, size):
        return pl.ds(pl.multiple_of(index * size, size), size)

    loads = [
        (qkv_hbm.at[0], qkv_ref),
        (table_hbm, table_ref),
        (gains_hbm.at[0], gains_ref),
        (owner_hbm, owner_ref),
        (plan_hbm, plan_ref),
        (gate_hbm.at[0], gate_ref),
    ]
    loads = [
        pltpu.make_async_copy(src, dst, local.at[3 + i]) for i, (src, dst) in enumerate(loads)
    ]
    for load in loads:
        load.start()

    barrier = pltpu.get_barrier_semaphore()

    def greet(where, section_=None):
        place = {"seq": where} if section_ is None else {"seq": where, "section": section_}
        pl.semaphore_signal(barrier, inc=1, device_id=place, device_id_type=MESH)

    @pl.loop(1, plane * CORES)
    def _(i):
        greet(x * plane * CORES + lax.rem(here + i, plane * CORES))

    for dx in range(1, nx):
        for c in range(CORES):
            greet(at((x + dx) % nx, yz, c))
    for x_ in range(nx):
        for c in range(CORES):
            greet(at(x_, yz, c), 1 - section)
    per_head = nx * CORES
    for m in range(CORES):
        source = at((seq % per_head) // CORES, seq // per_head, m)

        @pl.when(source != seq)
        def _():
            greet(source)

    text_dest = [yz * per_head + CORES * x + part for part in range(CORES)]
    to_self = sum((dest == seq).astype(jnp.int32) for dest in text_dest)

    for load in loads:
        load.wait()
    own = owner_ref[plan_ref[section * CORES + core]]
    own_core, own_yz, own_x = own % CORES, (own // CORES) % plane, own // (CORES * plane)
    own_y, own_z = own_yz // nz, own_yz % nz

    pl.semaphore_wait(
        barrier, plane * CORES - 1 + CORES * (nx - 1) + CORES * nx + CORES - to_self
    )

    order = (1, 2, 0)
    for t in order:
        remote(
            text_ref.at[0, other, 0, t], slots.at[core, t], t_send.at[0, t], t_recv.at[0, t],
            at(x, yz, other),
        )
        pltpu.make_async_copy(
            text_ref.at[0, core, 0, t], slots.at[core, t], t_local.at[t]
        ).start()

    def spread(t):
        drain(slots.at[0, t], t_recv.at[0, t])
        drain(slots.at[0, t], t_local.at[t])

        def fill(dst, row, count, lane, size):
            chunk = min(size, 512)

            @pl.loop(0, size // chunk)
            def _(k):
                span = pl.ds(pl.multiple_of(lane + k * chunk, HEAD), chunk)
                rows = pl.ds(pl.multiple_of(row, 16), count)
                dst[:, lanes(k, chunk)] = jnp.where(
                    own_core == 0, slots[0, t, rows, span], slots[1, t, rows, span]
                )

        for dx in sorted(range(nx), key=lambda d: -min(d, nx - d)):
            x_ = (x + dx) % nx
            if dx == 0:
                fill(a1[t].at[x], x_ * group, rows_a[t], 0, inner)
            else:
                fill(a1_out[t].at[dx - 1], x_ * group, rows_a[t], 0, inner)
                remote(
                    a1_out[t].at[dx - 1], a1[t].at[x], t_send.at[1, t], t_recv.at[1, t],
                    at(x_, yz, core),
                )

        @pl.loop(0, nx)
        def _(g):
            fill(b1_out[t].at[g], g * group + rows_a[t], rows_b[t], far * wide, wide)
            fill(b1[t].at[y, g], g * group + rows_a[t], rows_b[t], y * wide, wide)

        remote(
            b1_out[t], b1[t].at[y], t_send.at[2, t], t_recv.at[2, t],
            at(x, far * nz + z, core),
        )

    def cross(t):
        drain(a1[t].at[pl.ds(0, nx - 1)], t_recv.at[1, t])
        a2_out[t][...] = a1[t][own_x, :, lanes(far, wide)]
        remote(
            a2_out[t], a2[t].at[y], t_send.at[3, t], t_recv.at[3, t],
            at(x, far * nz + z, core),
        )
        a2[t][y] = a1[t][own_x, :, lanes(y, wide)]
        drain(b1[t].at[0], t_recv.at[2, t])
        for dx in sorted(range(nx), key=lambda d: -min(d, nx - d)):
            x_ = (x + dx) % nx
            if dx == 0:
                b2[t][x] = b1[t][own_y, x_]
            else:
                b2_out[t][dx - 1] = b1[t][own_y, x_]
                remote(
                    b2_out[t].at[dx - 1], b2[t].at[x], t_send.at[4, t], t_recv.at[4, t],
                    at(x_, yz, core),
                )

    def deal(t):
        drain(a2[t].at[0], t_recv.at[3, t])
        drain(b2[t].at[pl.ds(0, nx - 1)], t_recv.at[4, t])

        def fill(dst, z_):
            dst[pl.ds(0, rows_a[t]), :] = a2[t][own_y, :, lanes(z_, HEAD)]
            dst[pl.ds(rows_a[t], rows_b[t]), :] = b2[t][own_x, :, lanes(z_, HEAD)]

        fill(z_in[t].at[z], z)

        @pl.loop(1, nz)
        def _(dz):
            z_ = lax.rem(z + dz, nz)
            fill(z_out.at[t, z_], z_)
            remote(
                z_out.at[t, z_], z_in[t].at[z], t_send.at[5, t], t_recv.at[5, t],
                at(x, y * nz + z_, core),
            )

    def weights_start():
        for dx in range(nx):
            for dc in range(CORES):
                x_, c_ = (x + dx) % nx, (core + dc) % CORES
                columns = lanes(x_ * CORES + c_, width)
                weight_from, weight_to = weight_ref.at[0, :, columns], wts.at[z, y, block]
                if dx == 0 and dc == 0:
                    pltpu.make_async_copy(weight_from, weight_to, local.at[0]).start()
                else:
                    remote(weight_from, weight_to, send.at[0], recv.at[0], at(x_, yz, c_))

    def hidden_start():
        for dx in range(nx):
            for dc in range(CORES):
                x_, c_ = (x + dx) % nx, (core + dc) % CORES
                columns = lanes(x_ * CORES + c_, width)
                hidden_from, hidden_to = hidden_ref.at[0, :, :, columns], hid.at[block]
                if dx == 0 and dc == 0:
                    pltpu.make_async_copy(hidden_from, hidden_to, local.at[1]).start()
                else:
                    remote(hidden_from, hidden_to, send.at[1], recv.at[1], at(x_, yz, c_))

    def weights_over_y():
        drain(wts.at[0, 0, 0], local.at[0])
        drain(wts.at[0, 0, pl.ds(0, blocks - 1)], recv.at[0])
        remote(wts.at[z, y], wts.at[z, y], send.at[7], recv.at[7], at(x, far * nz + z, core))

    steps = (nz // 2, (nz - 1) // 2)

    def ring(step):
        if step == 0:
            drain(wts.at[0, 0], recv.at[7])
        for way, sign in enumerate((1, -1)):
            if 0 < step <= steps[way]:
                drain(wts.at[0], ring_recv.at[way, step - 1])
            if step < steps[way]:
                slot = lax.rem(z - sign * step + nz, nz)
                remote(
                    wts.at[slot], wts.at[slot], ring_send.at[way, step],
                    ring_recv.at[way, step], at(x, y * nz + lax.rem(z + sign + nz, nz), core),
                )

    def heads_start():
        @pl.loop(0, plane)
        def _(head):
            for m in range(CORES):
                dest = at(x, head, m)

                @pl.when(dest != seq)
                def _():
                    remote(
                        qkv_send.at[head, m], qkv_recv.at[here], send.at[2], recv.at[2], dest
                    )

                @pl.when(dest == seq)
                def _():
                    pltpu.make_async_copy(
                        qkv_send.at[head, m], qkv_recv.at[here], local.at[2]
                    ).start()

    def keys_start():
        drain(qkv_recv.at[pl.ds(0, plane * CORES - 1)], recv.at[2])
        drain(qkv_recv.at[0], local.at[2])
        for dx in range(1, nx):
            remote(
                qkv_recv.at[:, pl.ds(1, 2)], image_kv.at[x], send.at[4], recv.at[4],
                at((x + dx) % nx, yz, core),
            )
        pltpu.make_async_copy(
            qkv_recv.at[:, pl.ds(1, 2)], image_kv.at[x], local.at[2]
        ).start()

    weights_start()
    spread(order[0])
    first = seq * tokens
    row_line = first // COLS
    col_line = pl.multiple_of(table_ref.shape[1] - COLS + first % COLS, tokens)
    cosine = table_ref[0, pl.ds(row_line, 1), :] + table_ref[0, pl.ds(col_line, tokens), :]
    sine = table_ref[1, pl.ds(row_line, 1), :] + table_ref[1, pl.ds(col_line, tokens), :]
    even = lax.broadcasted_iota(jnp.int32, (tokens, HEAD), 1) % 2 == 0

    @pl.loop(0, plane)
    def _(head):
        span = lanes(head, HEAD)
        for m in range(CORES):
            for t in range(2):
                field = normalize(qkv_ref[m, t, :, span], gains_ref[t, :][None, :])
                swapped = jnp.where(
                    even, pltpu.roll(field, HEAD - 1, 1), pltpu.roll(field, 1, 1)
                )
                qkv_send[head, m, t] = (field * cosine + swapped * sine).astype(jnp.bfloat16)
            qkv_send[head, m, 2] = qkv_ref[m, 2, :, span]

    heads_start()
    weights_over_y()
    spread(order[1])
    spread(order[2])
    ring(0)
    cross(order[0])
    keys_start()
    ring(1)
    cross(order[1])
    ring(2)
    deal(order[0])
    cross(order[2])
    deal(order[1])
    deal(order[2])
    ring(3)

    def meet(queries, keys, values):
        scores = lax.dot_general(
            queries, keys, (((1,), (1,)), ((), ())), preferred_element_type=jnp.float32
        )
        weights = jnp.exp2(scores * scale)
        part = weights[:, :HEAD]
        for k in range(1, keys.shape[0] // HEAD):
            part = part + weights[:, k * HEAD : (k + 1) * HEAD]
        return (
            jnp.dot(weights.astype(jnp.bfloat16), values, preferred_element_type=jnp.float32),
            part,
        )

    image_rows = plane * CORES * tokens
    row_block = HEAD
    sources = row_block // tokens

    def image_queries(index):
        return qkv_recv[pl.ds(index * sources, sources), 0].reshape(row_block, HEAD)

    def image_pair(x_):
        return [image_kv[x_, :, t].reshape(image_rows, HEAD) for t in range(2)]

    drain(image_kv.at[pl.ds(0, nx - 1)], recv.at[4])
    drain(image_kv.at[0], local.at[2])

    @pl.loop(0, image_rows // row_block)
    def _(index):
        queries = image_queries(index)
        parts = [meet(queries, *image_pair(x_)) for x_ in range(nx)]
        rows = lanes(index, row_block)
        num[rows, :] = sum(p[0] for p in parts[1:]) + parts[0][0]
        den[rows, :] = sum(p[1] for p in parts[1:]) + parts[0][1]

    def text_rows_of(t):
        drain(z_in[t].at[pl.ds(0, nz - 1)], t_recv.at[5, t])
        return z_in[t][own_z]

    text_kv[x, 0] = normalize(text_rows_of(1), gains_ref[3, :][None, :]).astype(jnp.bfloat16)
    text_kv[x, 1] = text_rows_of(2)
    for dx in range(1, nx):
        remote(
            text_kv.at[x], text_kv.at[x], send.at[6], recv.at[6], at((x + dx) % nx, yz, core)
        )
    text_q[...] = normalize(text_rows_of(0), gains_ref[2, :][None, :]).astype(jnp.bfloat16)
    queries = text_q[...]
    text_parts = [meet(queries, *image_pair(x_)) for x_ in range(nx)]
    drain(text_kv.at[pl.ds(0, nx - 1)], recv.at[6])

    def quotient(numerator, denominator):
        return (numerator / jnp.sum(denominator, axis=-1, keepdims=True)).astype(jnp.bfloat16)

    pair_rows = CORES * tokens
    own_lanes = lanes(yz, HEAD)

    @pl.loop(0, image_rows // row_block)
    def _(index):
        rows = lanes(index, row_block)
        pair = [text_kv[:, t].reshape(nx * group, HEAD) for t in range(2)]
        more = meet(image_queries(index), *pair)
        rows_out[rows, :] = quotient(num[rows, :] + more[0], den[rows, :] + more[1])
        for k in range(row_block // pair_rows):
            there = index * (row_block // pair_rows) + k

            @pl.when(there != yz)
            def _():
                remote(
                    rows_out.at[lanes(there, pair_rows), :], attn.at[x, core, :, own_lanes],
                    send.at[9], recv.at[9], at(x, there, core),
                )

    attn[x, core, :, own_lanes] = rows_out[lanes(yz, pair_rows), :]
    hidden_start()

    text_pair = [text_kv[:, t].reshape(nx * group, HEAD) for t in range(2)]
    text_parts.append(meet(queries, *text_pair))
    text_rows = quotient(
        sum(p[0] for p in text_parts[1:]) + text_parts[0][0],
        sum(p[1] for p in text_parts[1:]) + text_parts[0][1],
    )
    for part, dest in enumerate(text_dest):
        text_send[part] = text_rows[part * half : (part + 1) * half, :]

        @pl.when(dest != seq)
        def _():
            remote(
                text_send.at[part], text_out_ref.at[0, 0, core], send.at[8], recv.at[8], dest
            )

        @pl.when(dest == seq)
        def _():
            pltpu.make_async_copy(
                text_send.at[part], text_out_ref.at[0, 0, core], local.at[0]
            ).start()

    drain(rows_out.at[pl.ds(0, (plane - 1) * pair_rows), :], recv.at[9])
    for dx in sorted(range(1, nx), key=lambda d: -min(d, nx - d)):
        remote(
            attn.at[x, core], attn.at[x, core], send.at[10], line_recv.at[0, dx],
            at((x + dx) % nx, yz, core),
        )
    remote(
        attn.at[x, core], attn.at[x, core], send.at[3], line_recv.at[1, 0], at(x, yz, other)
    )
    for dx in sorted(range(1, nx), key=lambda d: min(d, nx - d)):
        x_ = (x - dx + nx) % nx
        drain(attn.at[0, 0], line_recv.at[0, dx])
        remote(
            attn.at[x_, core], attn.at[x_, core], send.at[3], line_recv.at[1, dx],
            at(x, yz, other),
        )
    for dx in range(nx):
        drain(attn.at[0, 0], line_recv.at[1, dx])

    ring(steps[0])

    depth = inner // (nx * ny)
    total[...] = jnp.zeros_like(total)

    @pl.loop(0, nx * ny)
    def _(k):
        left = attn[:, :, :, lanes(k, depth)].reshape(blocks * pair_rows, depth)
        right = wts[:, k % ny, pl.ds((k // ny) * CORES, CORES)].reshape(depth, width)
        total[...] += jnp.dot(left, right, preferred_element_type=jnp.float32)

    drain(hid.at[0], local.at[1])
    drain(hid.at[pl.ds(0, blocks - 1)], recv.at[1])
    columns = lanes(block, width)

    @pl.loop(0, blocks)
    def _(dest):
        x_, c_ = dest // CORES, dest % CORES
        for m in range(CORES):
            gate_row = gate_ref[pl.ds(plan_ref[section * CORES + m], 1), columns]
            rows = lanes((x_ * CORES + m) * CORES + c_, tokens)
            out_send[dest, m] = (
                hid[dest, m].astype(jnp.float32) + gate_row * total[rows, :]
            ).astype(jnp.bfloat16)
        remote(
            out_send.at[dest], handed_ref.at[0, :, :, columns], send.at[11], recv.at[11],
            at(x_, yz, c_), 1 - section,
        )

    for t in range(3):
        drain(slots.at[0, t], t_send.at[0, t])
        drain(a1[t].at[pl.ds(0, nx - 1)], t_send.at[1, t])
        drain(b1[t].at[0], t_send.at[2, t])
        drain(a2[t].at[0], t_send.at[3, t])
        drain(b2[t].at[pl.ds(0, nx - 1)], t_send.at[4, t])
        drain(z_in[t].at[pl.ds(0, nz - 1)], t_send.at[5, t])
    for step in range(steps[0]):
        for way in range(2):
            if step < steps[way]:
                drain(wts.at[0], ring_send.at[way, step])
    drain(wts.at[0, 0, pl.ds(0, blocks - 1)], send.at[0])
    drain(hid.at[pl.ds(0, blocks - 1)], send.at[1])
    drain(qkv_recv.at[pl.ds(0, plane * CORES - 1)], send.at[2])
    drain(attn.at[:, 0], send.at[3])
    drain(image_kv.at[pl.ds(0, nx - 1)], send.at[4])
    drain(text_kv.at[pl.ds(0, nx - 1)], send.at[6])
    drain(wts.at[0, 0], send.at[7])
    drain(rows_out.at[pl.ds(0, (plane - 1) * pair_rows), :], send.at[9])
    drain(attn.at[pl.ds(0, nx - 1), 0], send.at[10])
    drain(out_send, send.at[11])

    @pl.when(to_self == 0)
    def _():
        drain(text_send, recv.at[8])
        drain(text_send, send.at[8])

    @pl.when(to_self != 0)
    def _():
        drain(text_send.at[0], recv.at[8])
        drain(text_send.at[0], local.at[0])
        drain(text_send.at[0], send.at[8])

    drain(out_send, recv.at[11])


def per_device(hidden, image_qkv, text_slots, norm_gains, out_weight, gate, owner, plan):
    nx, ny, nz = DIMS
    plane = ny * nz
    blocks = nx * CORES
    tokens, model = hidden.shape[2:]
    inner = image_qkv.shape[-1]
    text_len = text_slots.shape[4]
    group = text_len // nx
    split = [(rows, group - rows) for rows in (group * 3 // 4, group // 2, group // 2)]
    wide = inner // ny
    width = model // blocks
    weight_rows = out_weight.shape[1]
    image_rows = plane * CORES * tokens
    table = jnp.asarray(rope_table(tokens * blocks * plane))
    bf16, f32 = jnp.bfloat16, jnp.float32
    anywhere = pl.BlockSpec(memory_space=pl.ANY)
    dma = pltpu.SemaphoreType.DMA
    return pl.pallas_call(
        functools.partial(kernel, DIMS),
        out_shape=(
            jax.ShapeDtypeStruct(hidden.shape, bf16),
            jax.ShapeDtypeStruct((1, 1, CORES, group // CORES, HEAD), bf16),
        ),
        in_specs=[anywhere] * 9,
        out_specs=(anywhere, anywhere),
        scratch_shapes=[
            pltpu.SMEM(owner.shape, jnp.int32),
            pltpu.SMEM(plan.shape, jnp.int32),
            pltpu.VMEM(norm_gains.shape[1:], f32),
            pltpu.VMEM(table.shape, f32),
            pltpu.VMEM(gate.shape[1:], f32),
            pltpu.VMEM((CORES, 3, tokens, inner), bf16),
            pltpu.VMEM((CORES, 3, text_len, inner), bf16),
            *[pltpu.VMEM((nx - 1, a, inner), bf16) for a, _ in split],
            *[pltpu.VMEM((nx, a, inner), bf16) for a, _ in split],
            *[pltpu.VMEM((a, wide), bf16) for a, _ in split],
            *[pltpu.VMEM((ny, a, wide), bf16) for a, _ in split],
            *[pltpu.VMEM((nx, b, wide), bf16) for _, b in split],
            *[pltpu.VMEM((ny, nx, b, wide), bf16) for _, b in split],
            *[pltpu.VMEM((nx - 1, b, wide), bf16) for _, b in split],
            *[pltpu.VMEM((nx, b, wide), bf16) for _, b in split],
            pltpu.VMEM((3, nz, group, HEAD), bf16),
            *[pltpu.VMEM((nz, group, HEAD), bf16)] * 3,
            pltpu.VMEM((group, HEAD), bf16),
            pltpu.VMEM((nx, 2, group, HEAD), bf16),
            pltpu.VMEM((plane, CORES, 3, tokens, HEAD), bf16),
            pltpu.VMEM((plane * CORES, 3, tokens, HEAD), bf16),
            pltpu.VMEM((nx, plane * CORES, 2, tokens, HEAD), bf16),
            pltpu.VMEM((image_rows, HEAD), f32),
            pltpu.VMEM((image_rows, HEAD), f32),
            pltpu.VMEM((image_rows, HEAD), bf16),
            pltpu.VMEM((CORES, group // CORES, HEAD), bf16),
            pltpu.VMEM((nx, CORES, CORES * tokens, inner), bf16),
            pltpu.VMEM((nz, ny, blocks, weight_rows, width), bf16),
            pltpu.VMEM((blocks, CORES, tokens, width), bf16),
            pltpu.VMEM((blocks * CORES * tokens, width), f32),
            pltpu.VMEM((blocks, CORES, tokens, width), bf16),
            dma((12,)),
            dma((12,)),
            dma((12,)),
            dma((6, 3)),
            dma((6, 3)),
            dma((3,)),
            dma((2, nz // 2)),
            dma((2, nz // 2)),
            dma((2, nx)),
        ],
        compiler_params=pltpu.CompilerParams(
            collective_id=0, has_side_effects=True, vmem_limit_bytes=60 * 2**20
        ),
    )(
        owner,
        plan,
        norm_gains,
        table,
        gate,
        image_qkv.transpose(0, 1, 3, 2, 4),
        hidden,
        text_slots,
        out_weight,
    )


def solution(mesh):
    return jax.shard_map(
        per_device,
        mesh=mesh,
        in_specs=(
            P("section", None, "seq", None),
            P("section", None, "seq", None, None),
            P("section", None, "seq", None, None, None),
            P("section", None, None),
            P("section", "seq", None),
            P("section", None, None),
            P(),
            P(),
        ),
        out_specs=(P("section", None, "seq", None), P("section", "seq", None, None, None)),
        check_vma=False,
    )
```

```python
import functools
import math

import jax
import jax.numpy as jnp
import numpy as np
from jax import lax
from jax.experimental import pallas as pl
from jax.experimental.pallas import tpu as pltpu
from jax.sharding import PartitionSpec as P

COLS = 128
EPSILON = 1e-06
THETA = 10000.0
DIMS = (4, 2, 8)
CORES = 2
HEAD = 128
MESH = pl.DeviceIdType.MESH


def rope_table(tokens):
    rows = tokens // COLS
    time_dims = HEAD // 8
    space = (HEAD - time_dims) // 2
    frequency = np.exp(-math.log(THETA) * np.arange(0, space, 2) / space).astype(np.float32)

    def angles(count):
        at = np.arange(count, dtype=np.float32)[:, None] * frequency[None, :]
        return np.repeat(at.astype(np.float64), 2, axis=1)

    table = np.zeros((2, rows + COLS, HEAD), np.float32)
    sign = np.where(np.arange(space) % 2 == 0, -1.0, 1.0)
    table[0, :rows, :time_dims] = 1.0
    by_row = slice(time_dims, time_dims + space)
    by_col = slice(time_dims + space, HEAD)
    table[0, :rows, by_row] = np.cos(angles(rows))
    table[1, :rows, by_row] = np.sin(angles(rows)) * sign
    table[0, rows:, by_col] = np.cos(angles(COLS))
    table[1, rows:, by_col] = np.sin(angles(COLS)) * sign
    return table


def normalize(raw, gain):
    field = raw.astype(jnp.float32)
    return field * lax.rsqrt(jnp.mean(field * field, axis=-1, keepdims=True) + EPSILON) * gain


def drain(ref, sem):
    pltpu.make_async_copy(ref, ref, sem).wait()


def kernel(
    dims,
    owner_hbm,
    plan_hbm,
    gains_hbm,
    table_hbm,
    gate_hbm,
    qkv_hbm,
    hidden_ref,
    text_ref,
    weight_ref,
    handed_ref,
    text_out_ref,
    owner_ref,
    plan_ref,
    gains_ref,
    table_ref,
    gate_ref,
    qkv_ref,
    slots,
    a1_out_0,
    a1_out_1,
    a1_out_2,
    a1_0,
    a1_1,
    a1_2,
    a2_out_0,
    a2_out_1,
    a2_out_2,
    a2_0,
    a2_1,
    a2_2,
    b1_out_0,
    b1_out_1,
    b1_out_2,
    b1_0,
    b1_1,
    b1_2,
    b2_out_0,
    b2_out_1,
    b2_out_2,
    b2_0,
    b2_1,
    b2_2,
    z_out,
    z_in_0,
    z_in_1,
    z_in_2,
    text_q,
    text_kv,
    qkv_send,
    qkv_recv,
    image_kv,
    num,
    den,
    rows_out,
    text_send,
    attn,
    wts,
    hid,
    total,
    out_send,
    send,
    recv,
    local,
    t_send,
    t_recv,
    t_local,
    ring_send,
    ring_recv,
    line_recv,
):
    nx, ny, nz = dims
    plane = ny * nz
    seq = lax.axis_index("seq")
    section = lax.axis_index("section")
    core = seq % CORES
    yz = (seq // CORES) % plane
    x = seq // (CORES * plane)
    y, z = yz // nz, yz % nz
    other = CORES - 1 - core
    far = ny - 1 - y
    block = x * CORES + core
    blocks = nx * CORES
    here = yz * CORES + core
    tokens = qkv_ref.shape[2]
    group = text_q.shape[0]
    half = group // CORES
    a1, a2, b1, b2 = (a1_0, a1_1, a1_2), (a2_0, a2_1, a2_2), (b1_0, b1_1, b1_2), (b2_0, b2_1, b2_2)
    z_in = z_in_0, z_in_1, z_in_2
    a1_out, a2_out = (a1_out_0, a1_out_1, a1_out_2), (a2_out_0, a2_out_1, a2_out_2)
    b1_out, b2_out = (b1_out_0, b1_out_1, b1_out_2), (b2_out_0, b2_out_1, b2_out_2)
    rows_a, rows_b = [ref.shape[1] for ref in a1], [ref.shape[2] for ref in b1]
    wide = b1_0.shape[3]
    width = hid.shape[-1]
    inner = attn.shape[-1]
    scale = math.log2(math.e) / math.sqrt(HEAD)

    def at(x_, yz_, core_):
        return (x_ * plane + yz_) * CORES + core_

    def remote(src, dst, send_sem, recv_sem, where, section_=None):
        place = {"seq": where} if section_ is None else {"seq": where, "section": section_}
        pltpu.make_async_remote_copy(
            src_ref=src, dst_ref=dst, send_sem=send_sem, recv_sem=recv_sem,
            device_id=place, device_id_type=MESH,
        ).start()

    def lanes(index, size):
        return pl.ds(pl.multiple_of(index * size, size), size)

    loads = [
        (qkv_hbm.at[0], qkv_ref),
        (table_hbm, table_ref),
        (gains_hbm.at[0], gains_ref),
        (owner_hbm, owner_ref),
        (plan_hbm, plan_ref),
    ]
    loads = [
        pltpu.make_async_copy(src, dst, local.at[3 + i]) for i, (src, dst) in enumerate(loads)
    ]
    for load in loads:
        load.start()

    barrier = pltpu.get_barrier_semaphore()

    def greet(where, section_=None):
        place = {"seq": where} if section_ is None else {"seq": where, "section": section_}
        pl.semaphore_signal(barrier, inc=1, device_id=place, device_id_type=MESH)

    @pl.loop(1, plane * CORES)
    def _(i):
        greet(x * plane * CORES + lax.rem(here + i, plane * CORES))

    for dx in range(1, nx):
        for c in range(CORES):
            greet(at((x + dx) % nx, yz, c))
    for x_ in range(nx):
        for c in range(CORES):
            greet(at(x_, yz, c), 1 - section)

    @pl.loop(1, plane)
    def _(i):
        greet(at(x, lax.rem(yz + i, plane), core), 1 - section)

    per_head = nx * CORES
    for m in range(CORES):
        source = at((seq % per_head) // CORES, seq // per_head, m)

        @pl.when(source != seq)
        def _():
            greet(source)

    text_dest = [yz * per_head + CORES * x + part for part in range(CORES)]
    to_self = sum((dest == seq).astype(jnp.int32) for dest in text_dest)

    for load in loads:
        load.wait()
    own = owner_ref[plan_ref[section * CORES + core]]
    own_core, own_yz, own_x = own % CORES, (own // CORES) % plane, own // (CORES * plane)
    own_y, own_z = own_yz // nz, own_yz % nz

    pl.semaphore_wait(
        barrier, plane * CORES - 1 + CORES * (nx - 1) + CORES * nx + plane - 1 + CORES - to_self
    )

    order = (1, 2, 0)
    for t in order:
        remote(
            text_ref.at[0, other, 0, t], slots.at[core, t], t_send.at[0, t], t_recv.at[0, t],
            at(x, yz, other),
        )
        pltpu.make_async_copy(
            text_ref.at[0, core, 0, t], slots.at[core, t], t_local.at[t]
        ).start()

    def spread(t):
        drain(slots.at[0, t], t_recv.at[0, t])
        drain(slots.at[0, t], t_local.at[t])

        def fill(dst, row, count, lane, size):
            chunk = min(size, 512)

            @pl.loop(0, size // chunk)
            def _(k):
                span = pl.ds(pl.multiple_of(lane + k * chunk, HEAD), chunk)
                rows = pl.ds(pl.multiple_of(row, 16), count)
                dst[:, lanes(k, chunk)] = jnp.where(
                    own_core == 0, slots[0, t, rows, span], slots[1, t, rows, span]
                )

        for dx in sorted(range(nx), key=lambda d: -min(d, nx - d)):
            x_ = (x + dx) % nx
            if dx == 0:
                fill(a1[t].at[x], x_ * group, rows_a[t], 0, inner)
            else:
                fill(a1_out[t].at[dx - 1], x_ * group, rows_a[t], 0, inner)
                remote(
                    a1_out[t].at[dx - 1], a1[t].at[x], t_send.at[1, t], t_recv.at[1, t],
                    at(x_, yz, core),
                )

        @pl.loop(0, nx)
        def _(g):
            fill(b1_out[t].at[g], g * group + rows_a[t], rows_b[t], far * wide, wide)
            fill(b1[t].at[y, g], g * group + rows_a[t], rows_b[t], y * wide, wide)

        remote(
            b1_out[t], b1[t].at[y], t_send.at[2, t], t_recv.at[2, t],
            at(x, far * nz + z, core),
        )

    def cross(t):
        drain(a1[t].at[pl.ds(0, nx - 1)], t_recv.at[1, t])
        a2_out[t][...] = a1[t][own_x, :, lanes(far, wide)]
        remote(
            a2_out[t], a2[t].at[y], t_send.at[3, t], t_recv.at[3, t],
            at(x, far * nz + z, core),
        )
        a2[t][y] = a1[t][own_x, :, lanes(y, wide)]
        drain(b1[t].at[0], t_recv.at[2, t])
        for dx in sorted(range(nx), key=lambda d: -min(d, nx - d)):
            x_ = (x + dx) % nx
            if dx == 0:
                b2[t][x] = b1[t][own_y, x_]
            else:
                b2_out[t][dx - 1] = b1[t][own_y, x_]
                remote(
                    b2_out[t].at[dx - 1], b2[t].at[x], t_send.at[4, t], t_recv.at[4, t],
                    at(x_, yz, core),
                )

    def deal(t):
        drain(a2[t].at[0], t_recv.at[3, t])
        drain(b2[t].at[pl.ds(0, nx - 1)], t_recv.at[4, t])

        def fill(dst, z_):
            dst[pl.ds(0, rows_a[t]), :] = a2[t][own_y, :, lanes(z_, HEAD)]
            dst[pl.ds(rows_a[t], rows_b[t]), :] = b2[t][own_x, :, lanes(z_, HEAD)]

        fill(z_in[t].at[z], z)

        @pl.loop(1, nz)
        def _(dz):
            z_ = lax.rem(z + dz, nz)
            fill(z_out.at[t, z_], z_)
            remote(
                z_out.at[t, z_], z_in[t].at[z], t_send.at[5, t], t_recv.at[5, t],
                at(x, y * nz + z_, core),
            )

    def weights_start():
        for dx in range(nx):
            for dc in range(CORES):
                x_, c_ = (x + dx) % nx, (core + dc) % CORES
                columns = lanes(x_ * CORES + c_, width)
                remote(
                    weight_ref.at[0, :, columns], wts.at[z, y, block], send.at[0], recv.at[0],
                    at(x_, yz, c_), 1 - section,
                )
        remote(
            gate_hbm.at[0, :, lanes(block, width)], gate_ref, send.at[5], recv.at[5], seq,
            1 - section,
        )

    def hidden_start():
        for dx in range(nx):
            for dc in range(CORES):
                x_, c_ = (x + dx) % nx, (core + dc) % CORES
                columns = lanes(x_ * CORES + c_, width)
                remote(
                    hidden_ref.at[0, :, :, columns], hid.at[block], send.at[1], recv.at[1],
                    at(x_, yz, c_), 1 - section,
                )

    def weights_over_y():
        drain(wts.at[0, 0], recv.at[0])
        remote(wts.at[z, y], wts.at[z, y], send.at[7], recv.at[7], at(x, far * nz + z, core))

    steps = (nz // 2, (nz - 1) // 2)

    def ring(step):
        if step == 0:
            drain(wts.at[0, 0], recv.at[7])
        for way, sign in enumerate((1, -1)):
            if 0 < step <= steps[way]:
                drain(wts.at[0], ring_recv.at[way, step - 1])
            if step < steps[way]:
                slot = lax.rem(z - sign * step + nz, nz)
                remote(
                    wts.at[slot], wts.at[slot], ring_send.at[way, step],
                    ring_recv.at[way, step], at(x, y * nz + lax.rem(z + sign + nz, nz), core),
                )

    def heads_start():
        @pl.loop(0, plane)
        def _(head):
            for m in range(CORES):
                dest = at(x, head, m)

                @pl.when(dest != seq)
                def _():
                    remote(
                        qkv_send.at[head, m], qkv_recv.at[here], send.at[2], recv.at[2], dest
                    )

                @pl.when(dest == seq)
                def _():
                    pltpu.make_async_copy(
                        qkv_send.at[head, m], qkv_recv.at[here], local.at[2]
                    ).start()

    def keys_start():
        drain(qkv_recv.at[pl.ds(0, plane * CORES - 1)], recv.at[2])
        drain(qkv_recv.at[0], local.at[2])
        for dx in range(1, nx):
            remote(
                qkv_recv.at[:, pl.ds(1, 2)], image_kv.at[x], send.at[4], recv.at[4],
                at((x + dx) % nx, yz, core),
            )
        pltpu.make_async_copy(
            qkv_recv.at[:, pl.ds(1, 2)], image_kv.at[x], local.at[2]
        ).start()

    weights_start()
    spread(order[0])
    first = seq * tokens
    row_line = first // COLS
    col_line = pl.multiple_of(table_ref.shape[1] - COLS + first % COLS, tokens)
    cosine = table_ref[0, pl.ds(row_line, 1), :] + table_ref[0, pl.ds(col_line, tokens), :]
    sine = table_ref[1, pl.ds(row_line, 1), :] + table_ref[1, pl.ds(col_line, tokens), :]
    even = lax.broadcasted_iota(jnp.int32, (tokens, HEAD), 1) % 2 == 0

    @pl.loop(0, plane)
    def _(head):
        span = lanes(head, HEAD)
        for m in range(CORES):
            for t in range(2):
                field = normalize(qkv_ref[m, t, :, span], gains_ref[t, :][None, :])
                swapped = jnp.where(
                    even, pltpu.roll(field, HEAD - 1, 1), pltpu.roll(field, 1, 1)
                )
                qkv_send[head, m, t] = (field * cosine + swapped * sine).astype(jnp.bfloat16)
            qkv_send[head, m, 2] = qkv_ref[m, 2, :, span]

    heads_start()
    weights_over_y()
    spread(order[1])
    spread(order[2])
    ring(0)
    cross(order[0])
    keys_start()
    ring(1)
    cross(order[1])
    ring(2)
    deal(order[0])
    cross(order[2])
    deal(order[1])
    deal(order[2])
    ring(3)

    def meet(queries, keys, values):
        scores = lax.dot_general(
            queries, keys, (((1,), (1,)), ((), ())), preferred_element_type=jnp.float32
        )
        weights = jnp.exp2(scores * scale)
        part = weights[:, :HEAD]
        for k in range(1, keys.shape[0] // HEAD):
            part = part + weights[:, k * HEAD : (k + 1) * HEAD]
        return (
            jnp.dot(weights.astype(jnp.bfloat16), values, preferred_element_type=jnp.float32),
            part,
        )

    image_rows = plane * CORES * tokens
    row_block = HEAD
    sources = row_block // tokens

    def image_queries(index):
        return qkv_recv[pl.ds(index * sources, sources), 0].reshape(row_block, HEAD)

    def image_pair(x_):
        return [image_kv[x_, :, t].reshape(image_rows, HEAD) for t in range(2)]

    drain(image_kv.at[pl.ds(0, nx - 1)], recv.at[4])
    drain(image_kv.at[0], local.at[2])

    @pl.loop(0, image_rows // row_block)
    def _(index):
        queries = image_queries(index)
        parts = [meet(queries, *image_pair(x_)) for x_ in range(nx)]
        rows = lanes(index, row_block)
        num[rows, :] = sum(p[0] for p in parts[1:]) + parts[0][0]
        den[rows, :] = sum(p[1] for p in parts[1:]) + parts[0][1]

    def text_rows_of(t):
        drain(z_in[t].at[pl.ds(0, nz - 1)], t_recv.at[5, t])
        return z_in[t][own_z]

    text_kv[x, 0] = normalize(text_rows_of(1), gains_ref[3, :][None, :]).astype(jnp.bfloat16)
    text_kv[x, 1] = text_rows_of(2)
    for dx in range(1, nx):
        remote(
            text_kv.at[x], text_kv.at[x], send.at[6], recv.at[6], at((x + dx) % nx, yz, core)
        )
    text_q[...] = normalize(text_rows_of(0), gains_ref[2, :][None, :]).astype(jnp.bfloat16)
    queries = text_q[...]
    text_parts = [meet(queries, *image_pair(x_)) for x_ in range(nx)]
    drain(text_kv.at[pl.ds(0, nx - 1)], recv.at[6])

    def quotient(numerator, denominator):
        return (numerator / jnp.sum(denominator, axis=-1, keepdims=True)).astype(jnp.bfloat16)

    pair_rows = CORES * tokens
    own_lanes = lanes(yz, HEAD)

    @pl.loop(0, image_rows // row_block)
    def _(index):
        rows = lanes(index, row_block)
        pair = [text_kv[:, t].reshape(nx * group, HEAD) for t in range(2)]
        more = meet(image_queries(index), *pair)
        rows_out[rows, :] = quotient(num[rows, :] + more[0], den[rows, :] + more[1])
        for k in range(row_block // pair_rows):
            there = index * (row_block // pair_rows) + k

            remote(
                rows_out.at[lanes(there, pair_rows), :], attn.at[x, core, :, own_lanes],
                send.at[9], recv.at[9], at(x, there, core), 1 - section,
            )

    hidden_start()

    text_pair = [text_kv[:, t].reshape(nx * group, HEAD) for t in range(2)]
    text_parts.append(meet(queries, *text_pair))
    text_rows = quotient(
        sum(p[0] for p in text_parts[1:]) + text_parts[0][0],
        sum(p[1] for p in text_parts[1:]) + text_parts[0][1],
    )
    for part, dest in enumerate(text_dest):
        text_send[part] = text_rows[part * half : (part + 1) * half, :]

        @pl.when(dest != seq)
        def _():
            remote(
                text_send.at[part], text_out_ref.at[0, 0, core], send.at[8], recv.at[8], dest
            )

        @pl.when(dest == seq)
        def _():
            pltpu.make_async_copy(
                text_send.at[part], text_out_ref.at[0, 0, core], local.at[0]
            ).start()

    drain(rows_out, recv.at[9])
    for dx in sorted(range(1, nx), key=lambda d: -min(d, nx - d)):
        remote(
            attn.at[x, core], attn.at[x, core], send.at[10], line_recv.at[0, dx],
            at((x + dx) % nx, yz, core),
        )
    remote(
        attn.at[x, core], attn.at[x, core], send.at[3], line_recv.at[1, 0], at(x, yz, other)
    )
    for dx in sorted(range(1, nx), key=lambda d: min(d, nx - d)):
        x_ = (x - dx + nx) % nx
        drain(attn.at[0, 0], line_recv.at[0, dx])
        remote(
            attn.at[x_, core], attn.at[x_, core], send.at[3], line_recv.at[1, dx],
            at(x, yz, other),
        )
    for dx in range(nx):
        drain(attn.at[0, 0], line_recv.at[1, dx])

    ring(steps[0])

    depth = inner // (nx * ny)
    total[...] = jnp.zeros_like(total)

    @pl.loop(0, nx * ny)
    def _(k):
        left = attn[:, :, :, lanes(k, depth)].reshape(blocks * pair_rows, depth)
        right = wts[:, k % ny, pl.ds((k // ny) * CORES, CORES)].reshape(depth, width)
        total[...] += jnp.dot(left, right, preferred_element_type=jnp.float32)

    drain(hid, recv.at[1])
    drain(gate_ref, recv.at[5])
    columns = lanes(block, width)

    @pl.loop(0, blocks)
    def _(dest):
        x_, c_ = dest // CORES, dest % CORES
        for m in range(CORES):
            gate_row = gate_ref[pl.ds(plan_ref[(1 - section) * CORES + m], 1), :]
            rows = lanes((x_ * CORES + m) * CORES + c_, tokens)
            out_send[dest, m] = (
                hid[dest, m].astype(jnp.float32) + gate_row * total[rows, :]
            ).astype(jnp.bfloat16)

        @pl.when(dest != block)
        def _():
            remote(
                out_send.at[dest], handed_ref.at[0, :, :, columns], send.at[11], recv.at[11],
                at(x_, yz, c_),
            )

        @pl.when(dest == block)
        def _():
            pltpu.make_async_copy(
                out_send.at[dest], handed_ref.at[0, :, :, columns], local.at[1]
            ).start()

    for t in range(3):
        drain(slots.at[0, t], t_send.at[0, t])
        drain(a1[t].at[pl.ds(0, nx - 1)], t_send.at[1, t])
        drain(b1[t].at[0], t_send.at[2, t])
        drain(a2[t].at[0], t_send.at[3, t])
        drain(b2[t].at[pl.ds(0, nx - 1)], t_send.at[4, t])
        drain(z_in[t].at[pl.ds(0, nz - 1)], t_send.at[5, t])
    for step in range(steps[0]):
        for way in range(2):
            if step < steps[way]:
                drain(wts.at[0], ring_send.at[way, step])
    drain(wts.at[0, 0], send.at[0])
    drain(hid, send.at[1])
    drain(gate_ref, send.at[5])
    drain(qkv_recv.at[pl.ds(0, plane * CORES - 1)], send.at[2])
    drain(attn.at[:, 0], send.at[3])
    drain(image_kv.at[pl.ds(0, nx - 1)], send.at[4])
    drain(text_kv.at[pl.ds(0, nx - 1)], send.at[6])
    drain(wts.at[0, 0], send.at[7])
    drain(rows_out, send.at[9])
    drain(attn.at[pl.ds(0, nx - 1), 0], send.at[10])
    drain(out_send.at[pl.ds(0, blocks - 1)], send.at[11])
    drain(out_send.at[0], local.at[1])

    @pl.when(to_self == 0)
    def _():
        drain(text_send, recv.at[8])
        drain(text_send, send.at[8])

    @pl.when(to_self != 0)
    def _():
        drain(text_send.at[0], recv.at[8])
        drain(text_send.at[0], local.at[0])
        drain(text_send.at[0], send.at[8])

    drain(out_send.at[pl.ds(0, blocks - 1)], recv.at[11])


def per_device(hidden, image_qkv, text_slots, norm_gains, out_weight, gate, owner, plan):
    nx, ny, nz = DIMS
    plane = ny * nz
    blocks = nx * CORES
    tokens, model = hidden.shape[2:]
    inner = image_qkv.shape[-1]
    text_len = text_slots.shape[4]
    group = text_len // nx
    split = [(rows, group - rows) for rows in (group * 3 // 4, group // 2, group // 2)]
    wide = inner // ny
    width = model // blocks
    weight_rows = out_weight.shape[1]
    image_rows = plane * CORES * tokens
    table = jnp.asarray(rope_table(tokens * blocks * plane))
    bf16, f32 = jnp.bfloat16, jnp.float32
    anywhere = pl.BlockSpec(memory_space=pl.ANY)
    dma = pltpu.SemaphoreType.DMA
    return pl.pallas_call(
        functools.partial(kernel, DIMS),
        out_shape=(
            jax.ShapeDtypeStruct(hidden.shape, bf16),
            jax.ShapeDtypeStruct((1, 1, CORES, group // CORES, HEAD), bf16),
        ),
        in_specs=[anywhere] * 9,
        out_specs=(anywhere, anywhere),
        scratch_shapes=[
            pltpu.SMEM(owner.shape, jnp.int32),
            pltpu.SMEM(plan.shape, jnp.int32),
            pltpu.VMEM(norm_gains.shape[1:], f32),
            pltpu.VMEM(table.shape, f32),
            pltpu.VMEM((gate.shape[1], width), f32),
            pltpu.VMEM((CORES, 3, tokens, inner), bf16),
            pltpu.VMEM((CORES, 3, text_len, inner), bf16),
            *[pltpu.VMEM((nx - 1, a, inner), bf16) for a, _ in split],
            *[pltpu.VMEM((nx, a, inner), bf16) for a, _ in split],
            *[pltpu.VMEM((a, wide), bf16) for a, _ in split],
            *[pltpu.VMEM((ny, a, wide), bf16) for a, _ in split],
            *[pltpu.VMEM((nx, b, wide), bf16) for _, b in split],
            *[pltpu.VMEM((ny, nx, b, wide), bf16) for _, b in split],
            *[pltpu.VMEM((nx - 1, b, wide), bf16) for _, b in split],
            *[pltpu.VMEM((nx, b, wide), bf16) for _, b in split],
            pltpu.VMEM((3, nz, group, HEAD), bf16),
            *[pltpu.VMEM((nz, group, HEAD), bf16)] * 3,
            pltpu.VMEM((group, HEAD), bf16),
            pltpu.VMEM((nx, 2, group, HEAD), bf16),
            pltpu.VMEM((plane, CORES, 3, tokens, HEAD), bf16),
            pltpu.VMEM((plane * CORES, 3, tokens, HEAD), bf16),
            pltpu.VMEM((nx, plane * CORES, 2, tokens, HEAD), bf16),
            pltpu.VMEM((image_rows, HEAD), f32),
            pltpu.VMEM((image_rows, HEAD), f32),
            pltpu.VMEM((image_rows, HEAD), bf16),
            pltpu.VMEM((CORES, group // CORES, HEAD), bf16),
            pltpu.VMEM((nx, CORES, CORES * tokens, inner), bf16),
            pltpu.VMEM((nz, ny, blocks, weight_rows, width), bf16),
            pltpu.VMEM((blocks, CORES, tokens, width), bf16),
            pltpu.VMEM((blocks * CORES * tokens, width), f32),
            pltpu.VMEM((blocks, CORES, tokens, width), bf16),
            dma((12,)),
            dma((12,)),
            dma((12,)),
            dma((6, 3)),
            dma((6, 3)),
            dma((3,)),
            dma((2, nz // 2)),
            dma((2, nz // 2)),
            dma((2, nx)),
        ],
        compiler_params=pltpu.CompilerParams(
            collective_id=0, has_side_effects=True, vmem_limit_bytes=60 * 2**20
        ),
    )(
        owner,
        plan,
        norm_gains,
        table,
        gate,
        image_qkv.transpose(0, 1, 3, 2, 4),
        hidden,
        text_slots,
        out_weight,
    )


def solution(mesh):
    return jax.shard_map(
        per_device,
        mesh=mesh,
        in_specs=(
            P("section", None, "seq", None),
            P("section", None, "seq", None, None),
            P("section", None, "seq", None, None, None),
            P("section", None, None),
            P("section", "seq", None),
            P("section", None, None),
            P(),
            P(),
        ),
        out_specs=(P("section", None, "seq", None), P("section", "seq", None, None, None)),
        check_vma=False,
    )
```

```python
import functools
import math

import jax
import jax.numpy as jnp
import numpy as np
from jax import lax
from jax.experimental import pallas as pl
from jax.experimental.pallas import tpu as pltpu
from jax.sharding import PartitionSpec as P

COLS = 128
EPSILON = 1e-06
THETA = 10000.0
DIMS = (4, 2, 8)
CORES = 2
HEAD = 128
MESH = pl.DeviceIdType.MESH


def rope_table(tokens):
    rows = tokens // COLS
    time_dims = HEAD // 8
    space = (HEAD - time_dims) // 2
    frequency = np.exp(-math.log(THETA) * np.arange(0, space, 2) / space).astype(np.float32)

    def angles(count):
        at = np.arange(count, dtype=np.float32)[:, None] * frequency[None, :]
        return np.repeat(at.astype(np.float64), 2, axis=1)

    table = np.zeros((2, rows + COLS, HEAD), np.float32)
    sign = np.where(np.arange(space) % 2 == 0, -1.0, 1.0)
    table[0, :rows, :time_dims] = 1.0
    by_row = slice(time_dims, time_dims + space)
    by_col = slice(time_dims + space, HEAD)
    table[0, :rows, by_row] = np.cos(angles(rows))
    table[1, :rows, by_row] = np.sin(angles(rows)) * sign
    table[0, rows:, by_col] = np.cos(angles(COLS))
    table[1, rows:, by_col] = np.sin(angles(COLS)) * sign
    return table


def normalize(raw, gain):
    field = raw.astype(jnp.float32)
    return field * lax.rsqrt(jnp.mean(field * field, axis=-1, keepdims=True) + EPSILON) * gain


def drain(ref, sem):
    pltpu.make_async_copy(ref, ref, sem).wait()


def kernel(
    dims,
    owner_hbm,
    plan_hbm,
    gains_hbm,
    table_hbm,
    gate_hbm,
    qkv_hbm,
    hidden_ref,
    text_ref,
    weight_ref,
    handed_ref,
    text_out_ref,
    owner_ref,
    plan_ref,
    gains_ref,
    table_ref,
    gate_ref,
    qkv_ref,
    slots,
    a1_out_0,
    a1_out_1,
    a1_out_2,
    a1_0,
    a1_1,
    a1_2,
    a2_out_0,
    a2_out_1,
    a2_out_2,
    a2_0,
    a2_1,
    a2_2,
    b1_out_0,
    b1_out_1,
    b1_out_2,
    b1_0,
    b1_1,
    b1_2,
    b2_out_0,
    b2_out_1,
    b2_out_2,
    b2_0,
    b2_1,
    b2_2,
    z_out,
    z_in_0,
    z_in_1,
    z_in_2,
    text_q,
    text_kv,
    qkv_send,
    qkv_recv,
    image_kv,
    num,
    den,
    rows_out,
    text_send,
    attn,
    wts,
    hid,
    total,
    out_send,
    send,
    recv,
    local,
    t_send,
    t_recv,
    t_local,
    ring_send,
    ring_recv,
    line_recv,
):
    nx, ny, nz = dims
    plane = ny * nz
    seq = lax.axis_index("seq")
    section = lax.axis_index("section")
    core = seq % CORES
    yz = (seq // CORES) % plane
    x = seq // (CORES * plane)
    y, z = yz // nz, yz % nz
    other = CORES - 1 - core
    far = ny - 1 - y
    block = x * CORES + core
    blocks = nx * CORES
    here = yz * CORES + core
    tokens = qkv_ref.shape[2]
    group = text_q.shape[0]
    half = group // CORES
    a1, a2, b1, b2 = (a1_0, a1_1, a1_2), (a2_0, a2_1, a2_2), (b1_0, b1_1, b1_2), (b2_0, b2_1, b2_2)
    z_in = z_in_0, z_in_1, z_in_2
    a1_out, a2_out = (a1_out_0, a1_out_1, a1_out_2), (a2_out_0, a2_out_1, a2_out_2)
    b1_out, b2_out = (b1_out_0, b1_out_1, b1_out_2), (b2_out_0, b2_out_1, b2_out_2)
    rows_a, rows_b = [ref.shape[1] for ref in a1], [ref.shape[2] for ref in b1]
    wide = b1_0.shape[3]
    width = hid.shape[-1]
    inner = attn.shape[-1]
    scale = math.log2(math.e) / math.sqrt(HEAD)

    def at(x_, yz_, core_):
        return (x_ * plane + yz_) * CORES + core_

    def remote(src, dst, send_sem, recv_sem, where, section_=None):
        place = {"seq": where} if section_ is None else {"seq": where, "section": section_}
        pltpu.make_async_remote_copy(
            src_ref=src, dst_ref=dst, send_sem=send_sem, recv_sem=recv_sem,
            device_id=place, device_id_type=MESH,
        ).start()

    def lanes(index, size):
        return pl.ds(pl.multiple_of(index * size, size), size)

    loads = [
        (qkv_hbm.at[0], qkv_ref),
        (table_hbm, table_ref),
        (gains_hbm.at[0], gains_ref),
        (owner_hbm, owner_ref),
        (plan_hbm, plan_ref),
    ]
    loads = [
        pltpu.make_async_copy(src, dst, local.at[3 + i]) for i, (src, dst) in enumerate(loads)
    ]
    for load in loads:
        load.start()

    barrier = pltpu.get_barrier_semaphore()

    def greet(where, section_=None):
        place = {"seq": where} if section_ is None else {"seq": where, "section": section_}
        pl.semaphore_signal(barrier, inc=1, device_id=place, device_id_type=MESH)

    @pl.loop(1, plane * CORES)
    def _(i):
        greet(x * plane * CORES + lax.rem(here + i, plane * CORES))

    for dx in range(1, nx):
        for c in range(CORES):
            greet(at((x + dx) % nx, yz, c))
    for x_ in range(nx):
        for c in range(CORES):
            greet(at(x_, yz, c), 1 - section)

    @pl.loop(1, plane)
    def _(i):
        greet(at(x, lax.rem(yz + i, plane), core), 1 - section)

    per_head = nx * CORES
    for m in range(CORES):
        source = at((seq % per_head) // CORES, seq // per_head, m)

        @pl.when(source != seq)
        def _():
            greet(source)

    text_dest = [yz * per_head + CORES * x + part for part in range(CORES)]
    to_self = sum((dest == seq).astype(jnp.int32) for dest in text_dest)

    for load in loads:
        load.wait()
    own = owner_ref[plan_ref[section * CORES + core]]
    own_core, own_yz, own_x = own % CORES, (own // CORES) % plane, own // (CORES * plane)
    own_y, own_z = own_yz // nz, own_yz % nz

    pl.semaphore_wait(
        barrier, plane * CORES - 1 + CORES * (nx - 1) + CORES * nx + plane - 1 + CORES - to_self
    )

    order = (1, 2, 0)
    for t in order:
        remote(
            text_ref.at[0, other, 0, t], slots.at[core, t], t_send.at[0, t], t_recv.at[0, t],
            at(x, yz, other),
        )
        pltpu.make_async_copy(
            text_ref.at[0, core, 0, t], slots.at[core, t], t_local.at[t]
        ).start()

    def spread(t):
        drain(slots.at[0, t], t_recv.at[0, t])
        drain(slots.at[0, t], t_local.at[t])

        def fill(dst, row, count, lane, size):
            chunk = min(size, 512)

            @pl.loop(0, size // chunk)
            def _(k):
                span = pl.ds(pl.multiple_of(lane + k * chunk, HEAD), chunk)
                rows = pl.ds(pl.multiple_of(row, 16), count)
                dst[:, lanes(k, chunk)] = jnp.where(
                    own_core == 0, slots[0, t, rows, span], slots[1, t, rows, span]
                )

        for dx in sorted(range(nx), key=lambda d: -min(d, nx - d)):
            x_ = (x + dx) % nx
            if dx == 0:
                fill(a1[t].at[x], x_ * group, rows_a[t], 0, inner)
            else:
                fill(a1_out[t].at[dx - 1], x_ * group, rows_a[t], 0, inner)
                remote(
                    a1_out[t].at[dx - 1], a1[t].at[x], t_send.at[1, t], t_recv.at[1, t],
                    at(x_, yz, core),
                )

        @pl.loop(0, nx)
        def _(g):
            fill(b1_out[t].at[g], g * group + rows_a[t], rows_b[t], far * wide, wide)
            fill(b1[t].at[y, g], g * group + rows_a[t], rows_b[t], y * wide, wide)

        remote(
            b1_out[t], b1[t].at[y], t_send.at[2, t], t_recv.at[2, t],
            at(x, far * nz + z, core),
        )

    def cross(t):
        drain(a1[t].at[pl.ds(0, nx - 1)], t_recv.at[1, t])
        a2_out[t][...] = a1[t][own_x, :, lanes(far, wide)]
        remote(
            a2_out[t], a2[t].at[y], t_send.at[3, t], t_recv.at[3, t],
            at(x, far * nz + z, core),
        )
        a2[t][y] = a1[t][own_x, :, lanes(y, wide)]
        drain(b1[t].at[0], t_recv.at[2, t])
        for dx in sorted(range(nx), key=lambda d: -min(d, nx - d)):
            x_ = (x + dx) % nx
            if dx == 0:
                b2[t][x] = b1[t][own_y, x_]
            else:
                b2_out[t][dx - 1] = b1[t][own_y, x_]
                remote(
                    b2_out[t].at[dx - 1], b2[t].at[x], t_send.at[4, t], t_recv.at[4, t],
                    at(x_, yz, core),
                )

    def deal(t):
        drain(a2[t].at[0], t_recv.at[3, t])
        drain(b2[t].at[pl.ds(0, nx - 1)], t_recv.at[4, t])

        def fill(dst, z_):
            dst[pl.ds(0, rows_a[t]), :] = a2[t][own_y, :, lanes(z_, HEAD)]
            dst[pl.ds(rows_a[t], rows_b[t]), :] = b2[t][own_x, :, lanes(z_, HEAD)]

        fill(z_in[t].at[z], z)

        @pl.loop(1, nz)
        def _(dz):
            z_ = lax.rem(z + dz, nz)
            fill(z_out.at[t, z_], z_)
            remote(
                z_out.at[t, z_], z_in[t].at[z], t_send.at[5, t], t_recv.at[5, t],
                at(x, y * nz + z_, core),
            )

    def weights_start():
        for dx in range(nx):
            for dc in range(CORES):
                x_, c_ = (x + dx) % nx, (core + dc) % CORES
                columns = lanes(x_ * CORES + c_, width)
                remote(
                    weight_ref.at[0, :, columns], wts.at[z, y, block], send.at[0], recv.at[0],
                    at(x_, yz, c_), 1 - section,
                )
        remote(
            gate_hbm.at[0, :, lanes(block, width)], gate_ref, send.at[5], recv.at[5], seq,
            1 - section,
        )

    def hidden_start():
        for dx in range(nx):
            for dc in range(CORES):
                x_, c_ = (x + dx) % nx, (core + dc) % CORES
                columns = lanes(x_ * CORES + c_, width)
                remote(
                    hidden_ref.at[0, :, :, columns], hid.at[block], send.at[1], recv.at[1],
                    at(x_, yz, c_), 1 - section,
                )

    def weights_over_y():
        drain(wts.at[0, 0], recv.at[0])
        remote(wts.at[z, y], wts.at[z, y], send.at[7], recv.at[7], at(x, far * nz + z, core))

    steps = (nz // 2, (nz - 1) // 2)

    def ring(step):
        if step == 0:
            drain(wts.at[0, 0], recv.at[7])
        for way, sign in enumerate((1, -1)):
            if 0 < step <= steps[way]:
                drain(wts.at[0], ring_recv.at[way, step - 1])
            if step < steps[way]:
                slot = lax.rem(z - sign * step + nz, nz)
                remote(
                    wts.at[slot], wts.at[slot], ring_send.at[way, step],
                    ring_recv.at[way, step], at(x, y * nz + lax.rem(z + sign + nz, nz), core),
                )

    def heads_start():
        @pl.loop(0, plane)
        def _(head):
            for m in range(CORES):
                dest = at(x, head, m)

                @pl.when(dest != seq)
                def _():
                    remote(
                        qkv_send.at[head, m], qkv_recv.at[here], send.at[2], recv.at[2], dest
                    )

                @pl.when(dest == seq)
                def _():
                    pltpu.make_async_copy(
                        qkv_send.at[head, m], qkv_recv.at[here], local.at[2]
                    ).start()

    def keys_start():
        drain(qkv_recv.at[pl.ds(0, plane * CORES - 1)], recv.at[2])
        drain(qkv_recv.at[0], local.at[2])
        for dx, sem in ((1, recv.at[4]), (nx - 1, recv.at[3])):
            remote(
                qkv_recv.at[:, pl.ds(1, 2)], image_kv.at[x], send.at[4], sem,
                at((x + dx) % nx, yz, core),
            )
        pltpu.make_async_copy(
            qkv_recv.at[:, pl.ds(1, 2)], image_kv.at[x], local.at[2]
        ).start()

    def keys_forward():
        for dx, sem, part in ((1, recv.at[4], 0), (nx - 1, recv.at[3], 1)):
            drain(image_kv.at[0], sem)
            piece = image_kv.at[(x + nx - dx) % nx, pl.ds(part * plane, plane)]
            remote(piece, piece, send.at[4], recv.at[10], at((x + dx) % nx, yz, core))

    weights_start()
    spread(order[0])
    first = seq * tokens
    row_line = first // COLS
    col_line = pl.multiple_of(table_ref.shape[1] - COLS + first % COLS, tokens)
    cosine = table_ref[0, pl.ds(row_line, 1), :] + table_ref[0, pl.ds(col_line, tokens), :]
    sine = table_ref[1, pl.ds(row_line, 1), :] + table_ref[1, pl.ds(col_line, tokens), :]
    even = lax.broadcasted_iota(jnp.int32, (tokens, HEAD), 1) % 2 == 0

    @pl.loop(0, plane)
    def _(head):
        span = lanes(head, HEAD)
        for m in range(CORES):
            for t in range(2):
                field = normalize(qkv_ref[m, t, :, span], gains_ref[t, :][None, :])
                swapped = jnp.where(
                    even, pltpu.roll(field, HEAD - 1, 1), pltpu.roll(field, 1, 1)
                )
                qkv_send[head, m, t] = (field * cosine + swapped * sine).astype(jnp.bfloat16)
            qkv_send[head, m, 2] = qkv_ref[m, 2, :, span]

    heads_start()
    weights_over_y()
    spread(order[1])
    spread(order[2])
    ring(0)
    cross(order[0])
    keys_start()
    ring(1)
    cross(order[1])
    ring(2)
    deal(order[0])
    cross(order[2])
    keys_forward()
    deal(order[1])
    deal(order[2])
    ring(3)

    def meet(queries, keys, values):
        scores = lax.dot_general(
            queries, keys, (((1,), (1,)), ((), ())), preferred_element_type=jnp.float32
        )
        weights = jnp.exp2(scores * scale)
        part = weights[:, :HEAD]
        for k in range(1, keys.shape[0] // HEAD):
            part = part + weights[:, k * HEAD : (k + 1) * HEAD]
        return (
            jnp.dot(weights.astype(jnp.bfloat16), values, preferred_element_type=jnp.float32),
            part,
        )

    image_rows = plane * CORES * tokens
    row_block = HEAD
    sources = row_block // tokens

    def image_queries(index):
        return qkv_recv[pl.ds(index * sources, sources), 0].reshape(row_block, HEAD)

    def image_pair(x_):
        return [image_kv[x_, :, t].reshape(image_rows, HEAD) for t in range(2)]

    drain(image_kv.at[0], recv.at[10])
    drain(image_kv.at[0], local.at[2])

    @pl.loop(0, image_rows // row_block)
    def _(index):
        queries = image_queries(index)
        parts = [meet(queries, *image_pair(x_)) for x_ in range(nx)]
        rows = lanes(index, row_block)
        num[rows, :] = sum(p[0] for p in parts[1:]) + parts[0][0]
        den[rows, :] = sum(p[1] for p in parts[1:]) + parts[0][1]

    def text_rows_of(t):
        drain(z_in[t].at[pl.ds(0, nz - 1)], t_recv.at[5, t])
        return z_in[t][own_z]

    text_kv[x, 0] = normalize(text_rows_of(1), gains_ref[3, :][None, :]).astype(jnp.bfloat16)
    text_kv[x, 1] = text_rows_of(2)
    for dx in range(1, nx):
        remote(
            text_kv.at[x], text_kv.at[x], send.at[6], recv.at[6], at((x + dx) % nx, yz, core)
        )
    text_q[...] = normalize(text_rows_of(0), gains_ref[2, :][None, :]).astype(jnp.bfloat16)
    queries = text_q[...]
    text_parts = [meet(queries, *image_pair(x_)) for x_ in range(nx)]
    drain(text_kv.at[pl.ds(0, nx - 1)], recv.at[6])

    def quotient(numerator, denominator):
        return (numerator / jnp.sum(denominator, axis=-1, keepdims=True)).astype(jnp.bfloat16)

    pair_rows = CORES * tokens
    own_lanes = lanes(yz, HEAD)

    @pl.loop(0, image_rows // row_block)
    def _(index):
        rows = lanes(index, row_block)
        pair = [text_kv[:, t].reshape(nx * group, HEAD) for t in range(2)]
        more = meet(image_queries(index), *pair)
        rows_out[rows, :] = quotient(num[rows, :] + more[0], den[rows, :] + more[1])
        for k in range(row_block // pair_rows):
            there = index * (row_block // pair_rows) + k

            remote(
                rows_out.at[lanes(there, pair_rows), :], attn.at[x, core, :, own_lanes],
                send.at[9], recv.at[9], at(x, there, core), 1 - section,
            )

    hidden_start()

    text_pair = [text_kv[:, t].reshape(nx * group, HEAD) for t in range(2)]
    text_parts.append(meet(queries, *text_pair))
    text_rows = quotient(
        sum(p[0] for p in text_parts[1:]) + text_parts[0][0],
        sum(p[1] for p in text_parts[1:]) + text_parts[0][1],
    )
    for part, dest in enumerate(text_dest):
        text_send[part] = text_rows[part * half : (part + 1) * half, :]

        @pl.when(dest != seq)
        def _():
            remote(
                text_send.at[part], text_out_ref.at[0, 0, core], send.at[8], recv.at[8], dest
            )

        @pl.when(dest == seq)
        def _():
            pltpu.make_async_copy(
                text_send.at[part], text_out_ref.at[0, 0, core], local.at[0]
            ).start()

    drain(rows_out, recv.at[9])
    for dx in sorted(range(1, nx), key=lambda d: -min(d, nx - d)):
        remote(
            attn.at[x, core], attn.at[x, core], send.at[10], line_recv.at[0, dx],
            at((x + dx) % nx, yz, core),
        )
    remote(
        attn.at[x, core], attn.at[x, core], send.at[3], line_recv.at[1, 0], at(x, yz, other)
    )
    for dx in sorted(range(1, nx), key=lambda d: min(d, nx - d)):
        x_ = (x - dx + nx) % nx
        drain(attn.at[0, 0], line_recv.at[0, dx])
        remote(
            attn.at[x_, core], attn.at[x_, core], send.at[3], line_recv.at[1, dx],
            at(x, yz, other),
        )
    for dx in range(nx):
        drain(attn.at[0, 0], line_recv.at[1, dx])

    ring(steps[0])

    depth = inner // (nx * ny)
    total[...] = jnp.zeros_like(total)

    @pl.loop(0, nx * ny)
    def _(k):
        left = attn[:, :, :, lanes(k, depth)].reshape(blocks * pair_rows, depth)
        right = wts[:, k % ny, pl.ds((k // ny) * CORES, CORES)].reshape(depth, width)
        total[...] += jnp.dot(left, right, preferred_element_type=jnp.float32)

    drain(hid, recv.at[1])
    drain(gate_ref, recv.at[5])
    columns = lanes(block, width)

    @pl.loop(0, blocks)
    def _(dest):
        x_, c_ = dest // CORES, dest % CORES
        for m in range(CORES):
            gate_row = gate_ref[pl.ds(plan_ref[(1 - section) * CORES + m], 1), :]
            rows = lanes((x_ * CORES + m) * CORES + c_, tokens)
            out_send[dest, m] = (
                hid[dest, m].astype(jnp.float32) + gate_row * total[rows, :]
            ).astype(jnp.bfloat16)

        @pl.when(dest != block)
        def _():
            remote(
                out_send.at[dest], handed_ref.at[0, :, :, columns], send.at[11], recv.at[11],
                at(x_, yz, c_),
            )

        @pl.when(dest == block)
        def _():
            pltpu.make_async_copy(
                out_send.at[dest], handed_ref.at[0, :, :, columns], local.at[1]
            ).start()

    for t in range(3):
        drain(slots.at[0, t], t_send.at[0, t])
        drain(a1[t].at[pl.ds(0, nx - 1)], t_send.at[1, t])
        drain(b1[t].at[0], t_send.at[2, t])
        drain(a2[t].at[0], t_send.at[3, t])
        drain(b2[t].at[pl.ds(0, nx - 1)], t_send.at[4, t])
        drain(z_in[t].at[pl.ds(0, nz - 1)], t_send.at[5, t])
    for step in range(steps[0]):
        for way in range(2):
            if step < steps[way]:
                drain(wts.at[0], ring_send.at[way, step])
    drain(wts.at[0, 0], send.at[0])
    drain(hid, send.at[1])
    drain(gate_ref, send.at[5])
    drain(qkv_recv.at[pl.ds(0, plane * CORES - 1)], send.at[2])
    drain(attn.at[:, 0], send.at[3])
    drain(image_kv.at[pl.ds(0, nx - 1)], send.at[4])
    drain(text_kv.at[pl.ds(0, nx - 1)], send.at[6])
    drain(wts.at[0, 0], send.at[7])
    drain(rows_out, send.at[9])
    drain(attn.at[pl.ds(0, nx - 1), 0], send.at[10])
    drain(out_send.at[pl.ds(0, blocks - 1)], send.at[11])
    drain(out_send.at[0], local.at[1])

    @pl.when(to_self == 0)
    def _():
        drain(text_send, recv.at[8])
        drain(text_send, send.at[8])

    @pl.when(to_self != 0)
    def _():
        drain(text_send.at[0], recv.at[8])
        drain(text_send.at[0], local.at[0])
        drain(text_send.at[0], send.at[8])

    drain(out_send.at[pl.ds(0, blocks - 1)], recv.at[11])


def per_device(hidden, image_qkv, text_slots, norm_gains, out_weight, gate, owner, plan):
    nx, ny, nz = DIMS
    plane = ny * nz
    blocks = nx * CORES
    tokens, model = hidden.shape[2:]
    inner = image_qkv.shape[-1]
    text_len = text_slots.shape[4]
    group = text_len // nx
    split = [(rows, group - rows) for rows in (group * 3 // 4, group // 2, group // 2)]
    wide = inner // ny
    width = model // blocks
    weight_rows = out_weight.shape[1]
    image_rows = plane * CORES * tokens
    table = jnp.asarray(rope_table(tokens * blocks * plane))
    bf16, f32 = jnp.bfloat16, jnp.float32
    anywhere = pl.BlockSpec(memory_space=pl.ANY)
    dma = pltpu.SemaphoreType.DMA
    return pl.pallas_call(
        functools.partial(kernel, DIMS),
        out_shape=(
            jax.ShapeDtypeStruct(hidden.shape, bf16),
            jax.ShapeDtypeStruct((1, 1, CORES, group // CORES, HEAD), bf16),
        ),
        in_specs=[anywhere] * 9,
        out_specs=(anywhere, anywhere),
        scratch_shapes=[
            pltpu.SMEM(owner.shape, jnp.int32),
            pltpu.SMEM(plan.shape, jnp.int32),
            pltpu.VMEM(norm_gains.shape[1:], f32),
            pltpu.VMEM(table.shape, f32),
            pltpu.VMEM((gate.shape[1], width), f32),
            pltpu.VMEM((CORES, 3, tokens, inner), bf16),
            pltpu.VMEM((CORES, 3, text_len, inner), bf16),
            *[pltpu.VMEM((nx - 1, a, inner), bf16) for a, _ in split],
            *[pltpu.VMEM((nx, a, inner), bf16) for a, _ in split],
            *[pltpu.VMEM((a, wide), bf16) for a, _ in split],
            *[pltpu.VMEM((ny, a, wide), bf16) for a, _ in split],
            *[pltpu.VMEM((nx, b, wide), bf16) for _, b in split],
            *[pltpu.VMEM((ny, nx, b, wide), bf16) for _, b in split],
            *[pltpu.VMEM((nx - 1, b, wide), bf16) for _, b in split],
            *[pltpu.VMEM((nx, b, wide), bf16) for _, b in split],
            pltpu.VMEM((3, nz, group, HEAD), bf16),
            *[pltpu.VMEM((nz, group, HEAD), bf16)] * 3,
            pltpu.VMEM((group, HEAD), bf16),
            pltpu.VMEM((nx, 2, group, HEAD), bf16),
            pltpu.VMEM((plane, CORES, 3, tokens, HEAD), bf16),
            pltpu.VMEM((plane * CORES, 3, tokens, HEAD), bf16),
            pltpu.VMEM((nx, plane * CORES, 2, tokens, HEAD), bf16),
            pltpu.VMEM((image_rows, HEAD), f32),
            pltpu.VMEM((image_rows, HEAD), f32),
            pltpu.VMEM((image_rows, HEAD), bf16),
            pltpu.VMEM((CORES, group // CORES, HEAD), bf16),
            pltpu.VMEM((nx, CORES, CORES * tokens, inner), bf16),
            pltpu.VMEM((nz, ny, blocks, weight_rows, width), bf16),
            pltpu.VMEM((blocks, CORES, tokens, width), bf16),
            pltpu.VMEM((blocks * CORES * tokens, width), f32),
            pltpu.VMEM((blocks, CORES, tokens, width), bf16),
            dma((12,)),
            dma((12,)),
            dma((12,)),
            dma((6, 3)),
            dma((6, 3)),
            dma((3,)),
            dma((2, nz // 2)),
            dma((2, nz // 2)),
            dma((2, nx)),
        ],
        compiler_params=pltpu.CompilerParams(
            collective_id=0, has_side_effects=True, vmem_limit_bytes=60 * 2**20
        ),
    )(
        owner,
        plan,
        norm_gains,
        table,
        gate,
        image_qkv.transpose(0, 1, 3, 2, 4),
        hidden,
        text_slots,
        out_weight,
    )


def solution(mesh):
    return jax.shard_map(
        per_device,
        mesh=mesh,
        in_specs=(
            P("section", None, "seq", None),
            P("section", None, "seq", None, None),
            P("section", None, "seq", None, None, None),
            P("section", None, None),
            P("section", "seq", None),
            P("section", None, None),
            P(),
            P(),
        ),
        out_specs=(P("section", None, "seq", None), P("section", "seq", None, None, None)),
        check_vma=False,
    )
```

```python
import functools
import math

import jax
import jax.numpy as jnp
import numpy as np
from jax import lax
from jax.experimental import pallas as pl
from jax.experimental.pallas import tpu as pltpu
from jax.sharding import PartitionSpec as P

COLS = 128
EPSILON = 1e-06
THETA = 10000.0
DIMS = (4, 2, 8)
CORES = 2
HEAD = 128
MESH = pl.DeviceIdType.MESH


def rope_table(tokens):
    rows = tokens // COLS
    time_dims = HEAD // 8
    space = (HEAD - time_dims) // 2
    frequency = np.exp(-math.log(THETA) * np.arange(0, space, 2) / space).astype(np.float32)

    def angles(count):
        at = np.arange(count, dtype=np.float32)[:, None] * frequency[None, :]
        return np.repeat(at.astype(np.float64), 2, axis=1)

    table = np.zeros((2, rows + COLS, HEAD), np.float32)
    sign = np.where(np.arange(space) % 2 == 0, -1.0, 1.0)
    table[0, :rows, :time_dims] = 1.0
    by_row = slice(time_dims, time_dims + space)
    by_col = slice(time_dims + space, HEAD)
    table[0, :rows, by_row] = np.cos(angles(rows))
    table[1, :rows, by_row] = np.sin(angles(rows)) * sign
    table[0, rows:, by_col] = np.cos(angles(COLS))
    table[1, rows:, by_col] = np.sin(angles(COLS)) * sign
    return table


def normalize(raw, gain):
    field = raw.astype(jnp.float32)
    return field * lax.rsqrt(jnp.mean(field * field, axis=-1, keepdims=True) + EPSILON) * gain


def drain(ref, sem):
    pltpu.make_async_copy(ref, ref, sem).wait()


def kernel(
    dims,
    owner_hbm,
    plan_hbm,
    gains_hbm,
    table_hbm,
    gate_hbm,
    qkv_hbm,
    hidden_ref,
    text_ref,
    weight_ref,
    handed_ref,
    text_out_ref,
    owner_ref,
    plan_ref,
    gains_ref,
    table_ref,
    gate_ref,
    qkv_ref,
    slots,
    a1_out_0,
    a1_out_1,
    a1_out_2,
    a1_0,
    a1_1,
    a1_2,
    a2_out_0,
    a2_out_1,
    a2_out_2,
    a2_0,
    a2_1,
    a2_2,
    b1_out_0,
    b1_out_1,
    b1_out_2,
    b1_0,
    b1_1,
    b1_2,
    b2_out_0,
    b2_out_1,
    b2_out_2,
    b2_0,
    b2_1,
    b2_2,
    z_out,
    z_in_0,
    z_in_1,
    z_in_2,
    text_q,
    text_kv,
    qkv_send,
    qkv_recv,
    image_kv,
    num,
    den,
    rows_out,
    text_send,
    attn,
    wts,
    hid,
    total,
    out_send,
    send,
    recv,
    local,
    t_send,
    t_recv,
    t_local,
    ring_send,
    ring_recv,
    line_recv,
):
    nx, ny, nz = dims
    plane = ny * nz
    seq = lax.axis_index("seq")
    section = lax.axis_index("section")
    core = seq % CORES
    yz = (seq // CORES) % plane
    x = seq // (CORES * plane)
    y, z = yz // nz, yz % nz
    other = CORES - 1 - core
    far = ny - 1 - y
    block = x * CORES + core
    blocks = nx * CORES
    here = yz * CORES + core
    tokens = qkv_ref.shape[2]
    group = text_q.shape[0]
    half = group // CORES
    a1, a2, b1, b2 = (a1_0, a1_1, a1_2), (a2_0, a2_1, a2_2), (b1_0, b1_1, b1_2), (b2_0, b2_1, b2_2)
    z_in = z_in_0, z_in_1, z_in_2
    a1_out, a2_out = (a1_out_0, a1_out_1, a1_out_2), (a2_out_0, a2_out_1, a2_out_2)
    b1_out, b2_out = (b1_out_0, b1_out_1, b1_out_2), (b2_out_0, b2_out_1, b2_out_2)
    rows_a, rows_b = [ref.shape[1] for ref in a1], [ref.shape[2] for ref in b1]
    wide = b1_0.shape[3]
    width = hid.shape[-1]
    inner = attn.shape[-1]
    scale = math.log2(math.e) / math.sqrt(HEAD)

    def at(x_, yz_, core_):
        return (x_ * plane + yz_) * CORES + core_

    def remote(src, dst, send_sem, recv_sem, where, section_=None):
        place = {"seq": where} if section_ is None else {"seq": where, "section": section_}
        pltpu.make_async_remote_copy(
            src_ref=src, dst_ref=dst, send_sem=send_sem, recv_sem=recv_sem,
            device_id=place, device_id_type=MESH,
        ).start()

    def lanes(index, size):
        return pl.ds(pl.multiple_of(index * size, size), size)

    loads = [
        (qkv_hbm.at[0], qkv_ref),
        (table_hbm, table_ref),
        (gains_hbm.at[0], gains_ref),
        (owner_hbm, owner_ref),
        (plan_hbm, plan_ref),
    ]
    loads = [
        pltpu.make_async_copy(src, dst, local.at[3 + i]) for i, (src, dst) in enumerate(loads)
    ]
    for load in loads:
        load.start()

    barrier = pltpu.get_barrier_semaphore()

    def greet(where, section_=None):
        place = {"seq": where} if section_ is None else {"seq": where, "section": section_}
        pl.semaphore_signal(barrier, inc=1, device_id=place, device_id_type=MESH)

    @pl.loop(1, plane * CORES)
    def _(i):
        greet(x * plane * CORES + lax.rem(here + i, plane * CORES))

    for dx in range(1, nx):
        for c in range(CORES):
            greet(at((x + dx) % nx, yz, c))
    for x_ in range(nx):
        for c in range(CORES):
            greet(at(x_, yz, c), 1 - section)

    @pl.loop(1, plane)
    def _(i):
        greet(at(x, lax.rem(yz + i, plane), core), 1 - section)

    per_head = nx * CORES
    for m in range(CORES):
        source = at((seq % per_head) // CORES, seq // per_head, m)

        @pl.when(source != seq)
        def _():
            greet(source)

    text_dest = [yz * per_head + CORES * x + part for part in range(CORES)]
    to_self = sum((dest == seq).astype(jnp.int32) for dest in text_dest)

    for load in loads:
        load.wait()
    own = owner_ref[plan_ref[section * CORES + core]]
    own_core, own_yz, own_x = own % CORES, (own // CORES) % plane, own // (CORES * plane)
    own_y, own_z = own_yz // nz, own_yz % nz

    pl.semaphore_wait(
        barrier, plane * CORES - 1 + CORES * (nx - 1) + CORES * nx + plane - 1 + CORES - to_self
    )

    order = (1, 2, 0)
    for t in order:
        remote(
            text_ref.at[0, other, 0, t], slots.at[core, t], t_send.at[0, t], t_recv.at[0, t],
            at(x, yz, other),
        )
        pltpu.make_async_copy(
            text_ref.at[0, core, 0, t], slots.at[core, t], t_local.at[t]
        ).start()

    def spread(t):
        drain(slots.at[0, t], t_recv.at[0, t])
        drain(slots.at[0, t], t_local.at[t])

        def fill(dst, row, count, lane, size):
            chunk = min(size, 512)

            @pl.loop(0, size // chunk)
            def _(k):
                span = pl.ds(pl.multiple_of(lane + k * chunk, HEAD), chunk)
                rows = pl.ds(pl.multiple_of(row, 16), count)
                dst[:, lanes(k, chunk)] = jnp.where(
                    own_core == 0, slots[0, t, rows, span], slots[1, t, rows, span]
                )

        for dx in sorted(range(nx), key=lambda d: -min(d, nx - d)):
            x_ = (x + dx) % nx
            if dx == 0:
                fill(a1[t].at[x], x_ * group, rows_a[t], 0, inner)
            else:
                fill(a1_out[t].at[dx - 1], x_ * group, rows_a[t], 0, inner)
                remote(
                    a1_out[t].at[dx - 1], a1[t].at[x], t_send.at[1, t], t_recv.at[1, t],
                    at(x_, yz, core),
                )

        @pl.loop(0, nx)
        def _(g):
            fill(b1_out[t].at[g], g * group + rows_a[t], rows_b[t], far * wide, wide)
            fill(b1[t].at[y, g], g * group + rows_a[t], rows_b[t], y * wide, wide)

        remote(
            b1_out[t], b1[t].at[y], t_send.at[2, t], t_recv.at[2, t],
            at(x, far * nz + z, core),
        )

    def cross(t):
        drain(a1[t].at[pl.ds(0, nx - 1)], t_recv.at[1, t])
        a2_out[t][...] = a1[t][own_x, :, lanes(far, wide)]
        remote(
            a2_out[t], a2[t].at[y], t_send.at[3, t], t_recv.at[3, t],
            at(x, far * nz + z, core),
        )
        a2[t][y] = a1[t][own_x, :, lanes(y, wide)]
        drain(b1[t].at[0], t_recv.at[2, t])
        for dx in sorted(range(nx), key=lambda d: -min(d, nx - d)):
            x_ = (x + dx) % nx
            if dx == 0:
                b2[t][x] = b1[t][own_y, x_]
            else:
                b2_out[t][dx - 1] = b1[t][own_y, x_]
                remote(
                    b2_out[t].at[dx - 1], b2[t].at[x], t_send.at[4, t], t_recv.at[4, t],
                    at(x_, yz, core),
                )

    def deal(t):
        drain(a2[t].at[0], t_recv.at[3, t])
        drain(b2[t].at[pl.ds(0, nx - 1)], t_recv.at[4, t])

        def fill(dst, z_):
            dst[pl.ds(0, rows_a[t]), :] = a2[t][own_y, :, lanes(z_, HEAD)]
            dst[pl.ds(rows_a[t], rows_b[t]), :] = b2[t][own_x, :, lanes(z_, HEAD)]

        fill(z_in[t].at[z], z)

        @pl.loop(1, nz)
        def _(dz):
            z_ = lax.rem(z + dz, nz)
            fill(z_out.at[t, z_], z_)
            remote(
                z_out.at[t, z_], z_in[t].at[z], t_send.at[5, t], t_recv.at[5, t],
                at(x, y * nz + z_, core),
            )

    def weights_start():
        for dx in range(nx):
            for dc in range(CORES):
                x_, c_ = (x + dx) % nx, (core + dc) % CORES
                columns = lanes(x_ * CORES + c_, width)
                remote(
                    weight_ref.at[0, :, columns], wts.at[z, y, block], send.at[0], recv.at[0],
                    at(x_, yz, c_), 1 - section,
                )
        remote(
            gate_hbm.at[0, :, lanes(block, width)], gate_ref, send.at[5], recv.at[5], seq,
            1 - section,
        )

    def hidden_start():
        for dx in range(nx):
            for dc in range(CORES):
                x_, c_ = (x + dx) % nx, (core + dc) % CORES
                columns = lanes(x_ * CORES + c_, width)
                remote(
                    hidden_ref.at[0, :, :, columns], hid.at[block], send.at[1], recv.at[1],
                    at(x_, yz, c_), 1 - section,
                )

    def weights_over_y():
        drain(wts.at[0, 0], recv.at[0])
        remote(wts.at[z, y], wts.at[z, y], send.at[7], recv.at[7], at(x, far * nz + z, core))

    steps = (nz // 2, (nz - 1) // 2)

    def ring(step):
        if step == 0:
            drain(wts.at[0, 0], recv.at[7])
        for way, sign in enumerate((1, -1)):
            if 0 < step <= steps[way]:
                drain(wts.at[0], ring_recv.at[way, step - 1])
            if step < steps[way]:
                slot = lax.rem(z - sign * step + nz, nz)
                remote(
                    wts.at[slot], wts.at[slot], ring_send.at[way, step],
                    ring_recv.at[way, step], at(x, y * nz + lax.rem(z + sign + nz, nz), core),
                )

    def heads_start():
        @pl.loop(0, plane)
        def _(head):
            for m in range(CORES):
                dest = at(x, head, m)

                @pl.when(dest != seq)
                def _():
                    remote(
                        qkv_send.at[head, m], qkv_recv.at[here], send.at[2], recv.at[2], dest
                    )

                @pl.when(dest == seq)
                def _():
                    pltpu.make_async_copy(
                        qkv_send.at[head, m], qkv_recv.at[here], local.at[2]
                    ).start()

    def keys_start():
        drain(qkv_recv.at[pl.ds(0, plane * CORES - 1)], recv.at[2])
        drain(qkv_recv.at[0], local.at[2])
        for dx, sem in ((1, recv.at[4]), (nx - 1, recv.at[3])):
            remote(
                qkv_recv.at[:, pl.ds(1, 2)], image_kv.at[x], send.at[4], sem,
                at((x + dx) % nx, yz, core),
            )
        pltpu.make_async_copy(
            qkv_recv.at[:, pl.ds(1, 2)], image_kv.at[x], local.at[2]
        ).start()

    def keys_forward():
        for dx, sem, part in ((1, recv.at[4], 0), (nx - 1, recv.at[3], 1)):
            drain(image_kv.at[0], sem)
            piece = image_kv.at[(x + nx - dx) % nx, pl.ds(part * plane, plane)]
            remote(piece, piece, send.at[4], recv.at[10], at((x + dx) % nx, yz, core))

    weights_start()
    spread(order[0])
    first = seq * tokens
    row_line = first // COLS
    col_line = pl.multiple_of(table_ref.shape[1] - COLS + first % COLS, tokens)
    cosine = table_ref[0, pl.ds(row_line, 1), :] + table_ref[0, pl.ds(col_line, tokens), :]
    sine = table_ref[1, pl.ds(row_line, 1), :] + table_ref[1, pl.ds(col_line, tokens), :]
    even = lax.broadcasted_iota(jnp.int32, (tokens, HEAD), 1) % 2 == 0

    @pl.loop(0, plane)
    def _(head):
        span = lanes(head, HEAD)
        for m in range(CORES):
            for t in range(2):
                field = normalize(qkv_ref[m, t, :, span], gains_ref[t, :][None, :])
                swapped = jnp.where(
                    even, pltpu.roll(field, HEAD - 1, 1), pltpu.roll(field, 1, 1)
                )
                qkv_send[head, m, t] = (field * cosine + swapped * sine).astype(jnp.bfloat16)
            qkv_send[head, m, 2] = qkv_ref[m, 2, :, span]

    heads_start()
    weights_over_y()
    spread(order[1])
    spread(order[2])
    ring(0)
    cross(order[0])
    keys_start()
    ring(1)
    cross(order[1])
    ring(2)
    deal(order[0])
    cross(order[2])
    keys_forward()
    deal(order[1])
    deal(order[2])
    ring(3)

    def meet(queries, keys, values):
        scores = lax.dot_general(
            queries, keys, (((1,), (1,)), ((), ())), preferred_element_type=jnp.float32
        )
        weights = jnp.exp2(scores * scale)
        part = weights[:, :HEAD]
        for k in range(1, keys.shape[0] // HEAD):
            part = part + weights[:, k * HEAD : (k + 1) * HEAD]
        return (
            jnp.dot(weights.astype(jnp.bfloat16), values, preferred_element_type=jnp.float32),
            part,
        )

    image_rows = plane * CORES * tokens
    row_block = HEAD
    sources = row_block // tokens

    def image_queries(index):
        return qkv_recv[pl.ds(index * sources, sources), 0].reshape(row_block, HEAD)

    def image_pair(x_):
        return [image_kv[x_, :, t].reshape(image_rows, HEAD) for t in range(2)]

    def text_rows_of(t):
        drain(z_in[t].at[pl.ds(0, nz - 1)], t_recv.at[5, t])
        return z_in[t][own_z]

    text_kv[x, 0] = normalize(text_rows_of(1), gains_ref[3, :][None, :]).astype(jnp.bfloat16)
    text_kv[x, 1] = text_rows_of(2)
    for dx in range(1, nx):
        remote(
            text_kv.at[x], text_kv.at[x], send.at[6], recv.at[6], at((x + dx) % nx, yz, core)
        )

    drain(image_kv.at[0], recv.at[10])
    drain(image_kv.at[0], local.at[2])

    @pl.loop(0, image_rows // row_block)
    def _(index):
        queries = image_queries(index)
        parts = [meet(queries, *image_pair(x_)) for x_ in range(nx)]
        rows = lanes(index, row_block)
        num[rows, :] = sum(p[0] for p in parts[1:]) + parts[0][0]
        den[rows, :] = sum(p[1] for p in parts[1:]) + parts[0][1]

    text_q[...] = normalize(text_rows_of(0), gains_ref[2, :][None, :]).astype(jnp.bfloat16)
    queries = text_q[...]
    text_parts = [meet(queries, *image_pair(x_)) for x_ in range(nx)]
    drain(text_kv.at[pl.ds(0, nx - 1)], recv.at[6])

    def quotient(numerator, denominator):
        return (numerator / jnp.sum(denominator, axis=-1, keepdims=True)).astype(jnp.bfloat16)

    pair_rows = CORES * tokens
    own_lanes = lanes(yz, HEAD)

    @pl.loop(0, image_rows // row_block)
    def _(index):
        rows = lanes(index, row_block)
        pair = [text_kv[:, t].reshape(nx * group, HEAD) for t in range(2)]
        more = meet(image_queries(index), *pair)
        rows_out[rows, :] = quotient(num[rows, :] + more[0], den[rows, :] + more[1])
        for k in range(row_block // pair_rows):
            there = index * (row_block // pair_rows) + k

            remote(
                rows_out.at[lanes(there, pair_rows), :], attn.at[x, core, :, own_lanes],
                send.at[9], recv.at[9], at(x, there, core), 1 - section,
            )

    hidden_start()

    text_pair = [text_kv[:, t].reshape(nx * group, HEAD) for t in range(2)]
    text_parts.append(meet(queries, *text_pair))
    text_rows = quotient(
        sum(p[0] for p in text_parts[1:]) + text_parts[0][0],
        sum(p[1] for p in text_parts[1:]) + text_parts[0][1],
    )
    for part, dest in enumerate(text_dest):
        text_send[part] = text_rows[part * half : (part + 1) * half, :]

        @pl.when(dest != seq)
        def _():
            remote(
                text_send.at[part], text_out_ref.at[0, 0, core], send.at[8], recv.at[8], dest
            )

        @pl.when(dest == seq)
        def _():
            pltpu.make_async_copy(
                text_send.at[part], text_out_ref.at[0, 0, core], local.at[0]
            ).start()

    drain(rows_out, recv.at[9])
    for dx in sorted(range(1, nx), key=lambda d: -min(d, nx - d)):
        remote(
            attn.at[x, core], attn.at[x, core], send.at[10], line_recv.at[0, dx],
            at((x + dx) % nx, yz, core),
        )
    remote(
        attn.at[x, core], attn.at[x, core], send.at[3], line_recv.at[1, 0], at(x, yz, other)
    )
    for dx in sorted(range(1, nx), key=lambda d: min(d, nx - d)):
        x_ = (x - dx + nx) % nx
        drain(attn.at[0, 0], line_recv.at[0, dx])
        remote(
            attn.at[x_, core], attn.at[x_, core], send.at[3], line_recv.at[1, dx],
            at(x, yz, other),
        )
    for dx in range(nx):
        drain(attn.at[0, 0], line_recv.at[1, dx])

    ring(steps[0])

    depth = inner // (nx * ny)
    total[...] = jnp.zeros_like(total)

    @pl.loop(0, nx * ny)
    def _(k):
        left = attn[:, :, :, lanes(k, depth)].reshape(blocks * pair_rows, depth)
        right = wts[:, k % ny, pl.ds((k // ny) * CORES, CORES)].reshape(depth, width)
        total[...] += jnp.dot(left, right, preferred_element_type=jnp.float32)

    drain(hid, recv.at[1])
    drain(gate_ref, recv.at[5])
    columns = lanes(block, width)

    @pl.loop(0, blocks)
    def _(dest):
        x_, c_ = dest // CORES, dest % CORES
        for m in range(CORES):
            gate_row = gate_ref[pl.ds(plan_ref[(1 - section) * CORES + m], 1), :]
            rows = lanes((x_ * CORES + m) * CORES + c_, tokens)
            out_send[dest, m] = (
                hid[dest, m].astype(jnp.float32) + gate_row * total[rows, :]
            ).astype(jnp.bfloat16)

        @pl.when(dest != block)
        def _():
            remote(
                out_send.at[dest], handed_ref.at[0, :, :, columns], send.at[11], recv.at[11],
                at(x_, yz, c_),
            )

        @pl.when(dest == block)
        def _():
            pltpu.make_async_copy(
                out_send.at[dest], handed_ref.at[0, :, :, columns], local.at[1]
            ).start()

    for t in range(3):
        drain(slots.at[0, t], t_send.at[0, t])
        drain(a1[t].at[pl.ds(0, nx - 1)], t_send.at[1, t])
        drain(b1[t].at[0], t_send.at[2, t])
        drain(a2[t].at[0], t_send.at[3, t])
        drain(b2[t].at[pl.ds(0, nx - 1)], t_send.at[4, t])
        drain(z_in[t].at[pl.ds(0, nz - 1)], t_send.at[5, t])
    for step in range(steps[0]):
        for way in range(2):
            if step < steps[way]:
                drain(wts.at[0], ring_send.at[way, step])
    drain(wts.at[0, 0], send.at[0])
    drain(hid, send.at[1])
    drain(gate_ref, send.at[5])
    drain(qkv_recv.at[pl.ds(0, plane * CORES - 1)], send.at[2])
    drain(attn.at[:, 0], send.at[3])
    drain(image_kv.at[pl.ds(0, nx - 1)], send.at[4])
    drain(text_kv.at[pl.ds(0, nx - 1)], send.at[6])
    drain(wts.at[0, 0], send.at[7])
    drain(rows_out, send.at[9])
    drain(attn.at[pl.ds(0, nx - 1), 0], send.at[10])
    drain(out_send.at[pl.ds(0, blocks - 1)], send.at[11])
    drain(out_send.at[0], local.at[1])

    @pl.when(to_self == 0)
    def _():
        drain(text_send, recv.at[8])
        drain(text_send, send.at[8])

    @pl.when(to_self != 0)
    def _():
        drain(text_send.at[0], recv.at[8])
        drain(text_send.at[0], local.at[0])
        drain(text_send.at[0], send.at[8])

    drain(out_send.at[pl.ds(0, blocks - 1)], recv.at[11])


def per_device(hidden, image_qkv, text_slots, norm_gains, out_weight, gate, owner, plan):
    nx, ny, nz = DIMS
    plane = ny * nz
    blocks = nx * CORES
    tokens, model = hidden.shape[2:]
    inner = image_qkv.shape[-1]
    text_len = text_slots.shape[4]
    group = text_len // nx
    split = [(rows, group - rows) for rows in (group * 3 // 4, group // 2, group // 2)]
    wide = inner // ny
    width = model // blocks
    weight_rows = out_weight.shape[1]
    image_rows = plane * CORES * tokens
    table = jnp.asarray(rope_table(tokens * blocks * plane))
    bf16, f32 = jnp.bfloat16, jnp.float32
    anywhere = pl.BlockSpec(memory_space=pl.ANY)
    dma = pltpu.SemaphoreType.DMA
    return pl.pallas_call(
        functools.partial(kernel, DIMS),
        out_shape=(
            jax.ShapeDtypeStruct(hidden.shape, bf16),
            jax.ShapeDtypeStruct((1, 1, CORES, group // CORES, HEAD), bf16),
        ),
        in_specs=[anywhere] * 9,
        out_specs=(anywhere, anywhere),
        scratch_shapes=[
            pltpu.SMEM(owner.shape, jnp.int32),
            pltpu.SMEM(plan.shape, jnp.int32),
            pltpu.VMEM(norm_gains.shape[1:], f32),
            pltpu.VMEM(table.shape, f32),
            pltpu.VMEM((gate.shape[1], width), f32),
            pltpu.VMEM((CORES, 3, tokens, inner), bf16),
            pltpu.VMEM((CORES, 3, text_len, inner), bf16),
            *[pltpu.VMEM((nx - 1, a, inner), bf16) for a, _ in split],
            *[pltpu.VMEM((nx, a, inner), bf16) for a, _ in split],
            *[pltpu.VMEM((a, wide), bf16) for a, _ in split],
            *[pltpu.VMEM((ny, a, wide), bf16) for a, _ in split],
            *[pltpu.VMEM((nx, b, wide), bf16) for _, b in split],
            *[pltpu.VMEM((ny, nx, b, wide), bf16) for _, b in split],
            *[pltpu.VMEM((nx - 1, b, wide), bf16) for _, b in split],
            *[pltpu.VMEM((nx, b, wide), bf16) for _, b in split],
            pltpu.VMEM((3, nz, group, HEAD), bf16),
            *[pltpu.VMEM((nz, group, HEAD), bf16)] * 3,
            pltpu.VMEM((group, HEAD), bf16),
            pltpu.VMEM((nx, 2, group, HEAD), bf16),
            pltpu.VMEM((plane, CORES, 3, tokens, HEAD), bf16),
            pltpu.VMEM((plane * CORES, 3, tokens, HEAD), bf16),
            pltpu.VMEM((nx, plane * CORES, 2, tokens, HEAD), bf16),
            pltpu.VMEM((image_rows, HEAD), f32),
            pltpu.VMEM((image_rows, HEAD), f32),
            pltpu.VMEM((image_rows, HEAD), bf16),
            pltpu.VMEM((CORES, group // CORES, HEAD), bf16),
            pltpu.VMEM((nx, CORES, CORES * tokens, inner), bf16),
            pltpu.VMEM((nz, ny, blocks, weight_rows, width), bf16),
            pltpu.VMEM((blocks, CORES, tokens, width), bf16),
            pltpu.VMEM((blocks * CORES * tokens, width), f32),
            pltpu.VMEM((blocks, CORES, tokens, width), bf16),
            dma((12,)),
            dma((12,)),
            dma((12,)),
            dma((6, 3)),
            dma((6, 3)),
            dma((3,)),
            dma((2, nz // 2)),
            dma((2, nz // 2)),
            dma((2, nx)),
        ],
        compiler_params=pltpu.CompilerParams(
            collective_id=0, has_side_effects=True, vmem_limit_bytes=60 * 2**20
        ),
    )(
        owner,
        plan,
        norm_gains,
        table,
        gate,
        image_qkv.transpose(0, 1, 3, 2, 4),
        hidden,
        text_slots,
        out_weight,
    )


def solution(mesh):
    return jax.shard_map(
        per_device,
        mesh=mesh,
        in_specs=(
            P("section", None, "seq", None),
            P("section", None, "seq", None, None),
            P("section", None, "seq", None, None, None),
            P("section", None, None),
            P("section", "seq", None),
            P("section", None, None),
            P(),
            P(),
        ),
        out_specs=(P("section", None, "seq", None), P("section", "seq", None, None, None)),
        check_vma=False,
    )
```
